128 devices in a mesh: rep: 16 (over x_lo, y, core), exp: 8 (over x_hi, z).
Axes of the slice: x: 4 (x_hi: 2, x_lo: 2; x = x_hi * 2 + x_lo), y: 4, z: 4, core: 2. Of those that a mesh axis runs over, the one named last changes fastest.
Arguments:
- grad_out: bfloat16 [16384, 3072], P(('rep', 'exp')), may hold values from -6 to 6
- routes: int32 [16384, 2], P(('rep', 'exp')), may hold values from 0 to 7, all different within a row; in each aligned block of 128 rows (0 to 127, 128 to 255, ...) at most 36 rows name the same one
- probs: float32 [16384, 2], P(('rep', 'exp')), may hold values from 0.2 to 1
- rows_hidden: bfloat16 [8, 4608, 8192], P('exp', None, 'rep'), may hold values from -6 to 6
- w_down: bfloat16 [8, 8192, 3072], P('exp', 'rep'), may hold values from -0.0625 to 0.0625
Outputs:
- d_rows: bfloat16 [8, 4608, 8192], P('exp', None, 'rep')
- grad_down: bfloat16 [8, 8192, 3072], P('exp', 'rep')
The draws below stay inside these ranges and needn't reach their ends.
Inputs may be any that keep to these rules, and one draw needn't show every extreme that they name: The two experts of a token differ; within each device's block of 128 tokens no expert is named by more than 36 routes, a bound that some block reaches.
All inputs are finite; a program needn't handle non-finite values.
Results may differ from the reference program's by a relative error of at most 0.005.
Values may be sent and summed in bfloat16 or wider, within the bound.
A program may use at most 192 MiB of HBM per device.

```python
import math
import jax
import jax.numpy as jnp
import numpy as np
from jax import lax

D = 3072
EXPERTS = 8
TOK_DEV = 128
CAP = 36
FF = 8192
BLOCKS = 128
TOKENS = 16384


def level_of(key, shape, pieces, low, top_value):
    def one(dim, shards_of):
        steps = jax.random.uniform(jax.random.fold_in(jax.random.fold_in(key, 6), dim), (shards_of,), jnp.float32, low / len(pieces), top_value / len(pieces))
        return jnp.repeat(jnp.exp(steps), shape[dim] // shards_of).reshape((-1,) + (1,) * (len(shape) - dim - 1))

    level = one(*pieces[0])
    for cut in pieces[1:]:
        level = level * one(*cut)
    return level


def shared_out(own_key, own, number, rows, count, top, limit, slope):
    ranking = jax.random.permutation(own_key, count)
    heavy_load, common = load_shares(count, rows * top, limit, slope, True), load_shares(count, rows * top, limit, slope, False)
    places = jnp.arange(count)

    def named(lengths, offset_by):
        used = int((lengths > 0).sum())
        fixed = max(1, used // 4)
        moved = fixed + (places - fixed + offset_by * (used - fixed)) % max(1, count - fixed)
        return jnp.zeros((count,), jnp.int32).at[ranking[jnp.where(places < fixed, places, moved)]].set(jnp.asarray(lengths, jnp.int32))

    lengths = jnp.where(number % 4 == 0, named(heavy_load, number // 4), named(common, number - number // 4 - 1))
    mixed = jax.random.permutation(jax.random.fold_in(own, 3), count)
    donor, taker = mixed[0:count // 2 * 2:2], mixed[1:count // 2 * 2:2]
    slack = jnp.minimum(lengths[donor] - 1, limit - lengths[taker]) // 2
    slack = jnp.where((donor == ranking[0]) | (taker == ranking[0]) | (lengths[taker] == 0), 0, jnp.maximum(slack, 0))
    moved = jax.random.randint(jax.random.fold_in(own, 4), (count // 2,), 0, 1 << 20) % (slack + 1)
    lengths = lengths.at[donor].add(-moved).at[taker].add(moved)
    labels = jnp.searchsorted(jnp.cumsum(lengths), jnp.arange(rows * top), side="right").astype(jnp.int32)
    listing = labels.reshape(top, rows).T
    listing = listing[jax.random.permutation(jax.random.fold_in(own, 1), rows)]
    offset_by = jax.random.randint(jax.random.fold_in(own, 2), (rows, 1), 0, top)
    return jnp.take_along_axis(listing, (jnp.arange(top)[None, :] + offset_by) % top, axis=1)


def load_shares(count, total, reach, skew, full):
    portions = [(1 << 20) // math.isqrt(standing ** skew) + 1 for standing in range(1, count + 1)]
    largest = reach if full else min(reach, max(-(-total // count), total * portions[0] // sum(portions)))
    least = 1 if total - largest >= count - 1 else 0
    counts, surplus = [largest] + [least] * (count - 1), total - largest - least * (count - 1)
    while surplus > 0:
        candidates = [i for i in range(1, count) if counts[i] < largest] or [i for i in range(1, count) if counts[i] < reach]
        whole, left = sum([portions[i] for i in candidates]), surplus
        for i in candidates:
            addition = min(reach - counts[i], max(1, left * portions[i] // whole), surplus)
            counts[i] = counts[i] + addition
            surplus = surplus - addition
    return np.array(counts)


def bell_draw(rng, shape, scale, reach, shards=(), kind=jnp.bfloat16):
    array = jax.random.normal(rng, shape, jnp.float32) * scale
    if len(shards) > 0:
        array = level_of(rng, shape, shards, -0.22, 0.18) * array
    return jnp.clip(array, min=-reach, max=reach).astype(kind)


def setup_inputs(seed: int = 0) -> dict:
    splits = jax.random.split(jax.random.key(seed), 6)
    grad_out = bell_draw(splits[0], (TOKENS, D), 1.0, 6.0, ((0, 128),))
    routes_keys = jax.random.split(jax.random.fold_in(splits[1], 1), TOKENS // TOK_DEV)
    routes_turns = jax.random.permutation(jax.random.fold_in(splits[1], 3), TOKENS // TOK_DEV)
    routes = jax.vmap(lambda own, number: shared_out(jax.random.fold_in(splits[1], 2), own, number, TOK_DEV, EXPERTS, 2, CAP, 2))(routes_keys, routes_turns).reshape((TOKENS, 2))
    probs = jnp.clip(0.2 + 0.8 * jax.random.uniform(splits[2], (TOKENS, 2), jnp.float32) ** level_of(splits[2], (TOKENS, 2), ((0, 128),), -0.2, 0.2), 0.2, 1.0)
    rows_hidden = bell_draw(splits[3], (EXPERTS, BLOCKS * CAP, FF), 1.0, 6.0, ((0, 8), (2, 16)))
    w_down = bell_draw(splits[4], (EXPERTS, FF, D), FF ** -0.5, 0.0625, ((0, 8), (1, 16)))
    return dict(grad_out=grad_out, routes=routes, probs=probs, rows_hidden=rows_hidden, w_down=w_down)


def expert_grads(operands):
    cot_block, hid_block, wgt_down = operands
    d_rows = jnp.dot(cot_block, wgt_down.T, preferred_element_type=jnp.float32).astype(jnp.bfloat16)
    grad_down = jnp.dot(hid_block.T, cot_block, preferred_element_type=jnp.float32).astype(jnp.bfloat16)
    return d_rows, grad_down


def reference(grad_out, routes, probs, rows_hidden, w_down):
    devices_all = TOKENS // TOK_DEV
    route_rows = routes.reshape(devices_all, TOK_DEV * 2)
    onehot = (route_rows[:, :, None] == jnp.arange(EXPERTS, dtype=jnp.int32)[None, None, :]).astype(jnp.int32)
    before = jnp.cumsum(onehot, axis=1) - onehot
    slot_index = jnp.sum(before * onehot, axis=2)
    source = jnp.arange(devices_all, dtype=jnp.int32)[:, None]
    flat_index = ((route_rows * devices_all + source) * CAP + slot_index).reshape(TOKENS * 2).astype(jnp.int32)
    scaled = (probs.reshape(TOKENS * 2, 1) * jnp.repeat(grad_out, 2, axis=0).astype(jnp.float32)).astype(jnp.bfloat16)
    rows_dy = jnp.zeros((EXPERTS * devices_all * CAP, D), jnp.bfloat16).at[flat_index].set(scaled)
    rows_dy = rows_dy.reshape(EXPERTS, devices_all * CAP, D)
    d_rows, grad_down = lax.map(expert_grads, (rows_dy, rows_hidden, w_down))
    return d_rows, grad_down
```

```python
import jax
import jax.numpy as jnp
from jax import lax
from jax.experimental import pallas as pl
from jax.experimental.pallas import tpu as pltpu
from jax.sharding import PartitionSpec as P

CAP = 36
EXPERTS = 8
TOK = 128
D = 3072
FFD = 512
ROWS = 4608
W = 256
C = D // W
WIN = 48
GRP = 4 * CAP
UNIT = 2 * GRP
NU = 16
A = 160
A1 = 64
BR = UNIT - A
MESH = pl.DeviceIdType.MESH

LEXP, L1, L2, L3, LCORE = range(5)


def gather_kernel(
    rt_ref, pt_ref, g_hbm, h_hbm, w_hbm, d_hbm, gd_hbm,
    dy, send, recv, hb, ht, wv, gv, acc, gst, sel, prow,
    ssem, rsem, lsem, osem,
):
    rep = lax.axis_index("rep")
    ex = lax.axis_index("exp")
    lo, y, core = rep // 8, (rep // 2) % 4, rep % 2
    hi, z = ex // 4, ex % 4

    def unit(dl, dyy):
        return ((lo + dl) % 2 * 4 + (y + dyy + 4) % 4) * 2 + core

    to_x = (unit(1, 0), ex)
    to_yp = (unit(0, 1), ex)
    to_ym = (unit(0, -1), ex)
    to_core = ((lo * 4 + y) * 2 + 1 - core, ex)
    spread = []
    for dh in range(2):
        for dz in range(4):
            if dh or dz:
                hz = (hi + dh) % 2 * 4 + (z + dz) % 4
                spread.append((dh, (unit(dh, 0), hz), hz))
    peers = [to_x, to_yp, to_ym, to_core] + [s[1] for s in spread]

    load_g = pltpu.make_async_copy(g_hbm, gv, lsem.at[0])
    load_w = pltpu.make_async_copy(w_hbm.at[0], wv, lsem.at[1])
    load_g.start()

    bar = pltpu.get_barrier_semaphore()
    for p in peers:
        pl.semaphore_signal(bar, inc=1, device_id=p, device_id_type=MESH)

    def group_rows(i):
        u, part = i // 2, i % 2
        r = (u + 8 * part) % 16
        g = r * 2 + (hi + part) % 2
        return pl.multiple_of(g * GRP, 16)

    def start_hidden(i, _):
        pltpu.make_async_copy(
            h_hbm.at[0, pl.ds(group_rows(i), GRP)],
            hb.at[pl.ds(pl.multiple_of(i * GRP, 16), GRP)],
            lsem.at[2],
        ).start()
        return 0

    rt = rt_ref[...]
    pt = pt_ref[...]
    erow = lax.broadcasted_iota(jnp.int32, (EXPERTS, TOK), 0)
    oh0 = (rt[0:1] == erow).astype(jnp.float32)
    oh1 = (rt[1:2] == erow).astype(jnp.float32)
    upper = (
        lax.broadcasted_iota(jnp.int32, (TOK, TOK), 0)
        < lax.broadcasted_iota(jnp.int32, (TOK, TOK), 1)
    ).astype(jnp.float32)
    before = jnp.dot(oh0 + oh1, upper, preferred_element_type=jnp.float32)
    slot0 = jnp.sum(oh0 * before, axis=0, keepdims=True).astype(jnp.int32)
    slot1 = jnp.sum(oh1 * before, axis=0, keepdims=True).astype(jnp.int32)
    t0 = rt[0:1] * WIN + slot0 + 4 * z
    t1 = rt[1:2] * WIN + slot1 + 4 * z
    row = lax.broadcasted_iota(jnp.int32, (EXPERTS * WIN, TOK), 0)
    m0 = row == t0
    m1 = row == t1
    sel[...] = (m0 | m1).astype(jnp.float32).astype(jnp.bfloat16)
    pw = jnp.where(m0, pt[0:1], 0.0) + jnp.where(m1, pt[1:2], 0.0)
    prow[...] = jnp.broadcast_to(jnp.sum(pw, axis=1, keepdims=True), prow.shape)

    def remote(src, dst, stage, c, device):
        return pltpu.make_async_remote_copy(
            src_ref=src, dst_ref=dst, send_sem=ssem.at[stage, c], recv_sem=rsem.at[stage, c],
            device_id=device, device_id_type=MESH,
        )

    def wait_rows(sem, c, rows):
        ref = dy.at[c, pl.ds(0, rows)]
        pltpu.make_async_copy(ref, ref, sem).wait()

    def push(stage, c, u, start, rows, device):
        ref = dy.at[c, pl.ds(pl.multiple_of(u * UNIT + start, 16), rows)]
        remote(ref, ref, stage, c, device).start()

    def prep(c):
        g = gv[:, pl.ds(pl.multiple_of(c * W, W), W)]
        rows = jnp.dot(sel[...], g, preferred_element_type=jnp.float32)
        for i in range(W // 128):
            cols = slice(i * 128, (i + 1) * 128)
            send[c, :, cols] = (rows[:, cols] * prow[...]).astype(jnp.bfloat16)
        for dh, device, e in spread:
            remote(
                send.at[c, pl.ds(pl.multiple_of(e * WIN, 16), WIN)],
                recv.at[c, dh * 4 + z],
                LEXP, c, device,
            ).start()
        recv[c, z] = send[c, pl.ds(pl.multiple_of(ex * WIN, 16), WIN), :]

    def stage1(c):
        ref = recv.at[c, pl.ds(0, 7)]
        pltpu.make_async_copy(ref, ref, rsem.at[LEXP, c]).wait()
        base = rep * UNIT
        for part in range(2):
            for s in range(4):
                at = pl.multiple_of(base + part * GRP + s * 32, 16)
                if s == 0:
                    dy[c, pl.ds(at, 16), :] = recv[c, part * 4, 0:16, :]
                else:
                    dy[c, pl.ds(at, 16), :] = (
                        recv[c, part * 4 + s - 1, 32:48, :] + recv[c, part * 4 + s, 0:16, :]
                    )
                dy[c, pl.ds(pl.multiple_of(at + 16, 16), 16), :] = recv[c, part * 4 + s, 16:32, :]
                if s == 3:
                    dy[c, pl.ds(pl.multiple_of(at + 32, 16), 16), :] = recv[c, part * 4 + s, 32:48, :]
        for device in (to_x, to_yp, to_ym):
            push(L1, c, rep, 0, UNIT, device)
        push(LCORE, c, rep, 0, UNIT, to_core)

    def stage2(c):
        wait_rows(rsem.at[L1, c], c, 3 * UNIT)
        push(L2, c, unit(0, -1), 0, A, to_yp)
        push(L2, c, unit(0, 1), A, BR, to_ym)
        push(L2, c, unit(0, 1), A, BR, to_x)
        push(L2, c, unit(1, 0), 0, A, to_yp)
        push(L2, c, unit(1, 0), 0, A, to_ym)
        push(L2, c, unit(0, -1), A, BR, to_x)
        for u in (unit(1, 0), unit(0, 1), unit(0, -1)):
            push(LCORE, c, u, 0, UNIT, to_core)

    def stage3(c):
        wait_rows(rsem.at[L2, c], c, 3 * UNIT)
        push(L3, c, unit(1, -1), 0, A1, to_yp)
        push(L3, c, unit(1, 1), A1, A - A1, to_ym)
        push(L3, c, unit(0, 2), A, BR, to_x)
        for u in (unit(0, 2), unit(1, 1), unit(1, -1)):
            push(LCORE, c, u, 0, UNIT, to_core)

    def stage4(c):
        wait_rows(rsem.at[L3, c], c, UNIT)
        push(LCORE, c, unit(1, 2), 0, UNIT, to_core)

    def out_grad(c):
        return pltpu.make_async_copy(
            gst.at[c % 2],
            gd_hbm.at[0, :, pl.ds(pl.multiple_of(c * W, W), W)],
            osem.at[c % 2],
        )

    blk = 1152

    def d_block(c, i):
        at = pl.ds(pl.multiple_of(i * blk, blk), blk)
        wc = wv[:, pl.ds(pl.multiple_of(c * W, W), W)]
        return at, lax.dot_general(
            dy[c, at, :], wc, (((1,), (1,)), ((), ())), preferred_element_type=jnp.float32
        )

    def compute(c):
        wait_rows(rsem.at[LCORE, c], c, 8 * UNIT)

        @pl.when(c >= 2)
        def _():
            out_grad(c - 2).wait()

        gst[c % 2] = jnp.dot(ht[...], dy[c], preferred_element_type=jnp.float32).astype(jnp.bfloat16)
        out_grad(c).start()

        @pl.when(c < C - 1)
        def _():
            def body(i, _):
                at, part = d_block(c, i)
                acc[at, :] += part
                return 0

            lax.fori_loop(0, ROWS // blk, body, 0)

        @pl.when(c == C - 1)
        def _():
            def body(i, _):
                at, part = d_block(c, i)
                hb[at, :] = (acc[at, :] + part).astype(jnp.bfloat16)

                def put(k, _):
                    n = i * (blk // GRP) + k
                    pltpu.make_async_copy(
                        hb.at[pl.ds(pl.multiple_of(n * GRP, 16), GRP)],
                        d_hbm.at[0, pl.ds(group_rows(n), GRP)],
                        lsem.at[3],
                    ).start()
                    return 0

                lax.fori_loop(0, blk // GRP, put, 0)
                return 0

            lax.fori_loop(0, ROWS // blk, body, 0)

    load_g.wait()
    pl.semaphore_wait(bar, len(peers))
    prep(0)
    prep(1)
    lax.fori_loop(0, 32, start_hidden, 0)
    load_w.start()

    def turn_hidden():
        pltpu.make_async_copy(hb, hb, lsem.at[2]).wait()

        def body(i, _):
            at = pl.ds(pl.multiple_of(i * 128, 128), 128)
            ht[:, at] = hb[at, :].T
            return 0

        lax.fori_loop(0, ROWS // 128, body, 0)
        acc[...] = jnp.zeros_like(acc)
        load_w.wait()

    def step(t, _):
        def stage(lag, fn, ahead=0):
            c = t - lag + ahead

            @pl.when((c >= 0) & (c < C))
            def _():
                fn(c)

        stage(0, stage1)
        stage(1, stage2)
        stage(2, stage3)
        stage(3, stage4)

        @pl.when(t + 2 < C)
        def _():
            prep(t + 2)

        pl.when(t == 1)(turn_hidden)
        stage(4, compute)
        return 0

    lax.fori_loop(0, C + 4, step, 0)

    def drain(c, _):
        ref = recv.at[c, pl.ds(0, 7)]
        pltpu.make_async_copy(ref, ref, ssem.at[LEXP, c]).wait()
        wait_rows(ssem.at[L1, c], c, 3 * UNIT)
        wait_rows(ssem.at[L2, c], c, 3 * UNIT)
        wait_rows(ssem.at[L3, c], c, UNIT)
        wait_rows(ssem.at[LCORE, c], c, 8 * UNIT)
        return 0

    lax.fori_loop(0, C, drain, 0)
    out_grad(C - 2).wait()
    out_grad(C - 1).wait()
    pltpu.make_async_copy(hb, hb, lsem.at[3]).wait()


def per_device(grad_out, routes, probs, rows_hidden, w_down):
    bf = jnp.bfloat16
    any_spec = pl.BlockSpec(memory_space=pl.ANY)
    vmem = pl.BlockSpec(memory_space=pltpu.VMEM)
    return pl.pallas_call(
        gather_kernel,
        out_shape=(
            jax.ShapeDtypeStruct((1, ROWS, FFD), bf),
            jax.ShapeDtypeStruct((1, FFD, D), bf),
        ),
        in_specs=[vmem, vmem, any_spec, any_spec, any_spec],
        out_specs=(any_spec, any_spec),
        scratch_shapes=[
            pltpu.VMEM((C, ROWS, W), bf),
            pltpu.VMEM((C, EXPERTS * WIN, W), bf),
            pltpu.VMEM((C, 8, WIN, W), bf),
            pltpu.VMEM((ROWS, FFD), bf),
            pltpu.VMEM((FFD, ROWS), bf),
            pltpu.VMEM((FFD, D), bf),
            pltpu.VMEM((TOK, D), bf),
            pltpu.VMEM((ROWS, FFD), jnp.float32),
            pltpu.VMEM((2, FFD, W), bf),
            pltpu.VMEM((EXPERTS * WIN, TOK), bf),
            pltpu.VMEM((EXPERTS * WIN, 128), jnp.float32),
            pltpu.SemaphoreType.DMA((5, C)),
            pltpu.SemaphoreType.DMA((5, C)),
            pltpu.SemaphoreType.DMA((4,)),
            pltpu.SemaphoreType.DMA((2,)),
        ],
        compiler_params=pltpu.CompilerParams(
            collective_id=0, has_side_effects=True, vmem_limit_bytes=62 * 2**20
        ),
        cost_estimate=pl.CostEstimate(
            flops=4 * ROWS * D * FFD, bytes_accessed=2 * (2 * ROWS * FFD + 2 * FFD * D), transcendentals=0
        ),
    )(routes.T, probs.T, grad_out, rows_hidden, w_down)


def solution(mesh):
    return jax.shard_map(
        per_device,
        mesh=mesh,
        in_specs=(
            P(("rep", "exp"), None),
            P(("rep", "exp"), None),
            P(("rep", "exp"), None),
            P("exp", None, "rep"),
            P("exp", "rep", None),
        ),
        out_specs=(P("exp", None, "rep"), P("exp", "rep", None)),
        check_vma=False,
    )
```

```python
import jax
import jax.numpy as jnp
from jax import lax
from jax.experimental import pallas as pl
from jax.experimental.pallas import tpu as pltpu
from jax.sharding import PartitionSpec as P

CAP = 36
EXPERTS = 8
TOK = 128
D = 3072
FFD = 512
ROWS = 4608
LANES = 128
COLS = D // LANES
PAIRS = COLS // 2
NC = PAIRS + 2
WIN = 48
GRP = 4 * CAP
UNIT = 2 * GRP
NU = 16
A = 160
A1 = 64
BR = UNIT - A
MESH = pl.DeviceIdType.MESH

LEXP, L1, L2, L3, LC1, LC2, LC3, LC4 = range(8)
BLK = 4 * UNIT


def gather_kernel(
    rt_ref, pt_ref, g_hbm, h_hbm, w_hbm, d_out, gd_out,
    dy, send, recv, ht, wv, gv, acc, gacc, sel, prow,
    ssem, rsem, lsem,
):
    rep = lax.axis_index("rep")
    ex = lax.axis_index("exp")
    lo, y, core = rep // 8, (rep // 2) % 4, rep % 2
    hi, z = ex // 4, ex % 4
    hb = d_out.at[0]

    def unit(dl, dyy):
        return ((lo + dl) % 2 * 4 + (y + dyy + 4) % 4) * 2 + core

    to_x = (unit(1, 0), ex)
    to_yp = (unit(0, 1), ex)
    to_ym = (unit(0, -1), ex)
    to_core = ((lo * 4 + y) * 2 + 1 - core, ex)
    spread = []
    for dh in range(2):
        for dz in (2, 1, 3, 0):
            if dh or dz:
                hz = (hi + dh) % 2 * 4 + (z + dz) % 4
                spread.append((dh, (unit(dh, 0), hz), hz))
    peers = [to_x, to_yp, to_ym, to_core] + [s[1] for s in spread]

    load_g = pltpu.make_async_copy(g_hbm, gv, lsem.at[0])
    load_w = pltpu.make_async_copy(w_hbm.at[0], wv, lsem.at[1])
    load_g.start()

    bar = pltpu.get_barrier_semaphore()
    for p in peers:
        pl.semaphore_signal(bar, inc=1, device_id=p, device_id_type=MESH)

    def group_rows(i):
        u, part = i // 2, i % 2
        g = (u + 8 * part) % 16 * 2 + (hi + part) % 2
        return pl.ds(pl.multiple_of(g * GRP, 16), GRP)

    def local_rows(i):
        return pl.ds(pl.multiple_of(i * GRP, 16), GRP)

    def start_hidden(i, _):
        pltpu.make_async_copy(
            h_hbm.at[0, group_rows(i)], hb.at[local_rows(i)], lsem.at[2]
        ).start()
        return 0

    rt = rt_ref[...]
    pt = pt_ref[...]
    erow = lax.broadcasted_iota(jnp.int32, (EXPERTS, TOK), 0)
    oh0 = (rt[0:1] == erow).astype(jnp.float32)
    oh1 = (rt[1:2] == erow).astype(jnp.float32)
    upper = (
        lax.broadcasted_iota(jnp.int32, (TOK, TOK), 0)
        < lax.broadcasted_iota(jnp.int32, (TOK, TOK), 1)
    ).astype(jnp.float32)
    before = jnp.dot(oh0 + oh1, upper, preferred_element_type=jnp.float32)
    slot0 = jnp.sum(oh0 * before, axis=0, keepdims=True).astype(jnp.int32)
    slot1 = jnp.sum(oh1 * before, axis=0, keepdims=True).astype(jnp.int32)
    t0 = rt[0:1] * WIN + slot0 + 4 * z
    t1 = rt[1:2] * WIN + slot1 + 4 * z
    row = lax.broadcasted_iota(jnp.int32, (EXPERTS * WIN, TOK), 0)
    m0 = row == t0
    m1 = row == t1
    sel[...] = (m0 | m1).astype(jnp.float32).astype(jnp.bfloat16)
    pw = jnp.where(m0, pt[0:1], 0.0) + jnp.where(m1, pt[1:2], 0.0)
    prow[...] = jnp.broadcast_to(jnp.sum(pw, axis=1, keepdims=True), prow.shape)

    def tile0(c):
        return jnp.where(c < 2, c, jnp.where(c < NC - 2, 2 * c - 2, c + COLS - NC))

    def wide(c, fn):
        one = (c < 2) | (c >= NC - 2)

        @pl.when(one)
        def _():
            fn(c, 1)

        @pl.when(jnp.logical_not(one))
        def _():
            fn(c, 2)

    def remote(src, dst, stage, c, device):
        s = 0 if stage == LEXP else 1
        pltpu.make_async_remote_copy(
            src_ref=src, dst_ref=dst, send_sem=ssem.at[s, c], recv_sem=rsem.at[stage, c],
            device_id=device, device_id_type=MESH,
        ).start()

    def wait_rows(sem, c, n, rows):
        ref = dy.at[pl.ds(tile0(c), n), pl.ds(0, rows)]
        pltpu.make_async_copy(ref, ref, sem).wait()

    def wait_windows(sem, c, n):
        ref = recv.at[pl.ds(tile0(c), n), pl.ds(0, 7)]
        pltpu.make_async_copy(ref, ref, sem).wait()

    def push(stage, c, n, u, start, rows, device):
        ref = dy.at[pl.ds(tile0(c), n), pl.ds(pl.multiple_of(u * UNIT + start, 16), rows)]
        remote(ref, ref, stage, c, device)

    def make_windows(c, n):
        g = gv[:, pl.ds(pl.multiple_of(tile0(c) * LANES, LANES), n * LANES)]
        rows = jnp.dot(sel[...], g, preferred_element_type=jnp.float32)
        for i in range(n):
            tile = rows[:, i * LANES : (i + 1) * LANES] * prow[...]
            send[tile0(c) + i] = tile.astype(jnp.bfloat16)

    def send_windows(c, n):
        for dh, device, e in spread:
            remote(
                send.at[pl.ds(tile0(c), n), pl.ds(pl.multiple_of(e * WIN, 16), WIN)],
                recv.at[pl.ds(tile0(c), n), dh * 4 + z],
                LEXP, c, device,
            )
        for i in range(n):
            recv[tile0(c) + i, z] = send[tile0(c) + i, pl.ds(pl.multiple_of(ex * WIN, 16), WIN), :]

    def prep(c, n):
        make_windows(c, n)
        send_windows(c, n)

    def stage1(c, n):
        wait_windows(rsem.at[LEXP, c], c, n)
        for i in range(n):
            k = tile0(c) + i
            for part in range(2):
                for s in range(4):
                    at = rep * UNIT + part * GRP + s * 32
                    q = part * 4 + s
                    if s == 0:
                        first = recv[k, q, 0:16, :]
                    else:
                        first = recv[k, q - 1, 32:48, :] + recv[k, q, 0:16, :]
                    dy[k, pl.ds(pl.multiple_of(at, 16), 16), :] = first
                    dy[k, pl.ds(pl.multiple_of(at + 16, 16), 16), :] = recv[k, q, 16:32, :]
                    if s == 3:
                        dy[k, pl.ds(pl.multiple_of(at + 32, 16), 16), :] = recv[k, q, 32:48, :]
        for device in (to_x, to_yp, to_ym):
            push(L1, c, n, rep, 0, UNIT, device)
        push(LC1, c, n, rep, 0, UNIT, to_core)

    def stage2(c, n):
        wait_rows(rsem.at[L1, c], c, n, 3 * UNIT)
        push(L2, c, n, unit(0, -1), 0, A, to_yp)
        push(L2, c, n, unit(0, 1), A, BR, to_ym)
        push(L2, c, n, unit(0, 1), A, BR, to_x)
        push(L2, c, n, unit(1, 0), 0, A, to_yp)
        push(L2, c, n, unit(1, 0), 0, A, to_ym)
        push(L2, c, n, unit(0, -1), A, BR, to_x)
        for u in (unit(1, 0), unit(0, 1), unit(0, -1)):
            push(LC2, c, n, u, 0, UNIT, to_core)

    def stage3(c, n):
        wait_rows(rsem.at[L2, c], c, n, 3 * UNIT)
        push(L3, c, n, unit(1, -1), 0, A1, to_yp)
        push(L3, c, n, unit(1, 1), A1, A - A1, to_ym)
        push(L3, c, n, unit(0, 2), A, BR, to_x)
        for u in (unit(0, 2), unit(1, 1), unit(1, -1)):
            push(LC3, c, n, u, 0, UNIT, to_core)

    def stage4(c, n):
        wait_rows(rsem.at[L3, c], c, n, UNIT)
        push(LC4, c, n, unit(1, 2), 0, UNIT, to_core)

    def arrived(c, n):
        wait_rows(rsem.at[LC1, c], c, n, UNIT)
        wait_rows(rsem.at[LC2, c], c, n, 3 * UNIT)
        wait_rows(rsem.at[LC3, c], c, n, 3 * UNIT)
        wait_rows(rsem.at[LC4, c], c, n, UNIT)

    def multiply(k, b):
        at = pl.ds(pl.multiple_of(b * BLK, BLK), BLK)
        rows = jnp.concatenate([dy[2 * k, at, :], dy[2 * k + 1, at, :]], axis=1)
        wc = wv[:, pl.ds(pl.multiple_of(k * 2 * LANES, 2 * LANES), 2 * LANES)]
        gacc[...] += jnp.dot(ht[:, at], rows, preferred_element_type=jnp.float32)
        acc[at, :] += lax.dot_general(
            rows, wc, (((1,), (1,)), ((), ())), preferred_element_type=jnp.float32
        )

    def put_grad(k, grad):
        cols = pl.ds(pl.multiple_of(k * 2 * LANES, 2 * LANES), 2 * LANES)
        gd_out[0, :, cols] = grad.astype(jnp.bfloat16)

    def compute(k):
        rows = jnp.concatenate([dy[2 * k], dy[2 * k + 1]], axis=1)
        wc = wv[:, pl.ds(pl.multiple_of(k * 2 * LANES, 2 * LANES), 2 * LANES)]
        put_grad(k, jnp.dot(ht[...], rows, preferred_element_type=jnp.float32))
        acc[...] += lax.dot_general(
            rows, wc, (((1,), (1,)), ((), ())), preferred_element_type=jnp.float32
        )

    def finish(b):
        multiply(PAIRS - 1, b)

        def body(i, _):
            n = b * (BLK // GRP) + i
            d_out[0, group_rows(n), :] = acc[local_rows(n), :].astype(jnp.bfloat16)
            return 0

        lax.fori_loop(0, BLK // GRP, body, 0)

    def turn_hidden(part):
        def body(i, _):
            at = pl.ds(pl.multiple_of((part * 9 + i) * 128, 128), 128)
            ht[:, at] = hb[at, :].T
            return 0

        lax.fori_loop(0, 9, body, 0)
        at = pl.ds(pl.multiple_of(part * BLK, BLK), BLK)
        acc[at, :] = jnp.zeros((BLK, FFD), jnp.float32)

    load_g.wait()
    make_windows(0, 1)
    pl.semaphore_wait(bar, len(peers))
    send_windows(0, 1)
    lax.fori_loop(0, 32, start_hidden, 0)
    load_w.start()
    prep(1, 1)
    make_windows(2, 2)

    def step(t, _):
        def stage(lag, fn):
            c = t - lag

            @pl.when((c >= 0) & (c < NC))
            def _():
                wide(c, fn)

        stage(0, stage1)

        @pl.when(t == 0)
        def _():
            send_windows(2, 2)

        stage(1, stage2)
        stage(2, stage3)
        stage(3, stage4)

        @pl.when((t > 0) & (t + 2 < NC))
        def _():
            wide(t + 2, prep)

        @pl.when(t == 0)
        def _():
            pltpu.make_async_copy(hb, hb, lsem.at[2]).wait()
            load_w.wait()

        @pl.when(t < 4)
        def _():
            turn_hidden(t)

        stage(3, arrived)

        @pl.when((t >= 4) & (t < PAIRS + 3))
        def _():
            compute(t - 4)

        return 0

    lax.fori_loop(0, NC + 2, step, 0)

    last = NC - 1
    gacc[...] = jnp.zeros_like(gacc)
    wait_rows(rsem.at[LC1, last], last, 1, UNIT)
    wait_rows(rsem.at[LC2, last], last, 1, 3 * UNIT)
    wait_rows(rsem.at[LC3, last], last, 1, 3 * UNIT)
    late = (1 - lo) * 2 + (y + 2) % 4 // 2

    def tail(i, _):
        @pl.when(i == 2)
        def _():
            stage4(last, 1)

        @pl.when(i == 3)
        def _():
            wait_rows(rsem.at[LC4, last], last, 1, UNIT)

        finish((late + 1 + i) % 4)
        return 0

    lax.fori_loop(0, 4, tail, 0)
    put_grad(PAIRS - 1, gacc[...])

    def drain(c, _):
        def one(c, n):
            wait_windows(ssem.at[0, c], c, n)
            wait_rows(ssem.at[1, c], c, n, 15 * UNIT)

        wide(c, one)
        return 0

    lax.fori_loop(0, NC, drain, 0)


def store_kernel(d_in, gd_in, d_hbm, gd_hbm, sem):
    d = pltpu.make_async_copy(d_in, d_hbm, sem.at[0])
    g = pltpu.make_async_copy(gd_in, gd_hbm, sem.at[1])
    d.start()
    g.start()
    d.wait()
    g.wait()


def per_device(grad_out, routes, probs, rows_hidden, w_down):
    bf = jnp.bfloat16
    any_spec = pl.BlockSpec(memory_space=pl.ANY)
    vmem = pl.BlockSpec(memory_space=pltpu.VMEM)
    d_shape, gd_shape = (1, ROWS, FFD), (1, FFD, D)
    d_rows, grad = pl.pallas_call(
        gather_kernel,
        out_shape=(pltpu.VMEM(d_shape, bf), pltpu.VMEM(gd_shape, bf)),
        in_specs=[vmem, vmem, any_spec, any_spec, any_spec],
        out_specs=(vmem, vmem),
        scratch_shapes=[
            pltpu.VMEM((COLS, ROWS, LANES), bf),
            pltpu.VMEM((COLS, EXPERTS * WIN, LANES), bf),
            pltpu.VMEM((COLS, 8, WIN, LANES), bf),
            pltpu.VMEM((FFD, ROWS), bf),
            pltpu.VMEM((FFD, D), bf),
            pltpu.VMEM((TOK, D), bf),
            pltpu.VMEM((ROWS, FFD), jnp.float32),
            pltpu.VMEM((FFD, 2 * LANES), jnp.float32),
            pltpu.VMEM((EXPERTS * WIN, TOK), bf),
            pltpu.VMEM((EXPERTS * WIN, LANES), jnp.float32),
            pltpu.SemaphoreType.DMA((2, NC)),
            pltpu.SemaphoreType.DMA((8, NC)),
            pltpu.SemaphoreType.DMA((3,)),
        ],
        compiler_params=pltpu.CompilerParams(
            collective_id=0, has_side_effects=True, vmem_limit_bytes=54 * 2**20
        ),
        cost_estimate=pl.CostEstimate(
            flops=4 * ROWS * D * FFD, bytes_accessed=2 * (2 * ROWS * FFD + 2 * FFD * D), transcendentals=0
        ),
    )(routes.T, probs.T, grad_out, rows_hidden, w_down)
    return pl.pallas_call(
        store_kernel,
        out_shape=(jax.ShapeDtypeStruct(d_shape, bf), jax.ShapeDtypeStruct(gd_shape, bf)),
        in_specs=[vmem, vmem],
        out_specs=(any_spec, any_spec),
        scratch_shapes=[pltpu.SemaphoreType.DMA((2,))],
        compiler_params=pltpu.CompilerParams(vmem_limit_bytes=2 * 2**20),
    )(
        pltpu.with_memory_space_constraint(d_rows, pltpu.VMEM),
        pltpu.with_memory_space_constraint(grad, pltpu.VMEM),
    )


def solution(mesh):
    return jax.shard_map(
        per_device,
        mesh=mesh,
        in_specs=(
            P(("rep", "exp"), None),
            P(("rep", "exp"), None),
            P(("rep", "exp"), None),
            P("exp", None, "rep"),
            P("exp", "rep", None),
        ),
        out_specs=(P("exp", None, "rep"), P("exp", "rep", None)),
        check_vma=False,
    )
```

```python
import jax
import jax.numpy as jnp
from jax import lax
from jax.experimental import pallas as pl
from jax.experimental.pallas import tpu as pltpu
from jax.sharding import PartitionSpec as P

CAP = 36
EXPERTS = 8
TOK = 128
D = 3072
FFD = 512
ROWS = 4608
LANES = 128
COLS = D // LANES
PAIRS = COLS // 2
HEAD, TAIL = 2, 2
NC = HEAD + (COLS - HEAD - TAIL) // 2 + TAIL
WIN = 48
GRP = 4 * CAP
UNIT = 2 * GRP
NU = 16
A = 160
A1 = 64
BR = UNIT - A
MESH = pl.DeviceIdType.MESH

LEXP, L1, L2, L3, LC1, LC2, LC3, LC4 = range(8)
BLK = 4 * UNIT


def gather_kernel(
    rt_hbm, pt_hbm, g_hbm, h_hbm, w_hbm, d_out, gd_out,
    rt_ref, pt_ref, dy, send, recv, ht, wv, gv, acc, gacc, sel, prow,
    ssem, rsem, lsem,
):
    rep = lax.axis_index("rep")
    ex = lax.axis_index("exp")
    lo, y, core = rep // 8, (rep // 2) % 4, rep % 2
    hi, z = ex // 4, ex % 4
    hb = d_out.at[0]

    def unit(dl, dyy):
        return ((lo + dl) % 2 * 4 + (y + dyy + 4) % 4) * 2 + core

    to_x = (unit(1, 0), ex)
    to_yp = (unit(0, 1), ex)
    to_ym = (unit(0, -1), ex)
    to_core = ((lo * 4 + y) * 2 + 1 - core, ex)
    spread = []
    for dh in range(2):
        for dz in (2, 1, 3, 0):
            if dh or dz:
                hz = (hi + dh) % 2 * 4 + (z + dz) % 4
                spread.append((dh, (unit(dh, 0), hz), hz))
    peers = [to_x, to_yp, to_ym, to_core] + [s[1] for s in spread]

    load_g = pltpu.make_async_copy(g_hbm, gv, lsem.at[0])
    load_w = pltpu.make_async_copy(w_hbm.at[0], wv, lsem.at[1])
    load_r = pltpu.make_async_copy(rt_hbm, rt_ref, lsem.at[3])
    load_p = pltpu.make_async_copy(pt_hbm, pt_ref, lsem.at[4])
    load_r.start()
    load_p.start()
    load_g.start()

    bar = pltpu.get_barrier_semaphore()
    for p in peers:
        pl.semaphore_signal(bar, inc=1, device_id=p, device_id_type=MESH)

    def group_rows(i):
        u, part = i // 2, i % 2
        g = (u + 8 * part) % 16 * 2 + (hi + part) % 2
        return pl.ds(pl.multiple_of(g * GRP, 16), GRP)

    def local_rows(i):
        return pl.ds(pl.multiple_of(i * GRP, 16), GRP)

    def start_hidden(i, _):
        pltpu.make_async_copy(
            h_hbm.at[0, group_rows(i)], hb.at[local_rows(i)], lsem.at[2]
        ).start()
        return 0

    load_r.wait()
    load_p.wait()
    rt = rt_ref[...]
    pt = pt_ref[...]
    erow = lax.broadcasted_iota(jnp.int32, (EXPERTS, TOK), 0)
    oh0 = (rt[0:1] == erow).astype(jnp.float32)
    oh1 = (rt[1:2] == erow).astype(jnp.float32)
    upper = (
        lax.broadcasted_iota(jnp.int32, (TOK, TOK), 0)
        < lax.broadcasted_iota(jnp.int32, (TOK, TOK), 1)
    ).astype(jnp.float32)
    before = jnp.dot(oh0 + oh1, upper, preferred_element_type=jnp.float32)
    slot0 = jnp.sum(oh0 * before, axis=0, keepdims=True).astype(jnp.int32)
    slot1 = jnp.sum(oh1 * before, axis=0, keepdims=True).astype(jnp.int32)
    t0 = rt[0:1] * WIN + slot0 + 4 * z
    t1 = rt[1:2] * WIN + slot1 + 4 * z
    row = lax.broadcasted_iota(jnp.int32, (EXPERTS * WIN, TOK), 0)
    m0 = row == t0
    m1 = row == t1
    sel[...] = (m0 | m1).astype(jnp.float32).astype(jnp.bfloat16)
    pw = jnp.where(m0, pt[0:1], 0.0) + jnp.where(m1, pt[1:2], 0.0)
    prow[...] = jnp.broadcast_to(jnp.sum(pw, axis=1, keepdims=True), prow.shape)

    def tile0(c):
        return jnp.where(c < HEAD, c, jnp.where(c < NC - TAIL, 2 * c - HEAD, c + COLS - NC))

    def wide(c, fn):
        one = (c < HEAD) | (c >= NC - TAIL)

        @pl.when(one)
        def _():
            fn(c, 1)

        @pl.when(jnp.logical_not(one))
        def _():
            fn(c, 2)

    def remote(src, dst, stage, c, device):
        s = 0 if stage == LEXP else 1
        pltpu.make_async_remote_copy(
            src_ref=src, dst_ref=dst, send_sem=ssem.at[s, c], recv_sem=rsem.at[stage, c],
            device_id=device, device_id_type=MESH,
        ).start()

    def wait_rows(sem, c, n, rows):
        ref = dy.at[pl.ds(tile0(c), n), pl.ds(0, rows)]
        pltpu.make_async_copy(ref, ref, sem).wait()

    def wait_windows(sem, c, n):
        ref = recv.at[pl.ds(tile0(c), n), pl.ds(0, 7)]
        pltpu.make_async_copy(ref, ref, sem).wait()

    def push(stage, c, n, u, start, rows, device):
        ref = dy.at[pl.ds(tile0(c), n), pl.ds(pl.multiple_of(u * UNIT + start, 16), rows)]
        remote(ref, ref, stage, c, device)

    def make_windows(c, n):
        g = gv[:, pl.ds(pl.multiple_of(tile0(c) * LANES, LANES), n * LANES)]
        rows = jnp.dot(sel[...], g, preferred_element_type=jnp.float32)
        for i in range(n):
            tile = rows[:, i * LANES : (i + 1) * LANES] * prow[...]
            send[tile0(c) + i] = tile.astype(jnp.bfloat16)

    def send_windows(c, n):
        for dh, device, e in spread:
            remote(
                send.at[pl.ds(tile0(c), n), pl.ds(pl.multiple_of(e * WIN, 16), WIN)],
                recv.at[pl.ds(tile0(c), n), dh * 4 + z],
                LEXP, c, device,
            )
        for i in range(n):
            recv[tile0(c) + i, z] = send[tile0(c) + i, pl.ds(pl.multiple_of(ex * WIN, 16), WIN), :]

    def prep(c, n):
        make_windows(c, n)
        send_windows(c, n)

    def stage1(c, n):
        wait_windows(rsem.at[LEXP, c], c, n)
        for i in range(n):
            k = tile0(c) + i
            for part in range(2):
                for s in range(4):
                    at = rep * UNIT + part * GRP + s * 32
                    q = part * 4 + s
                    if s == 0:
                        first = recv[k, q, 0:16, :]
                    else:
                        first = recv[k, q - 1, 32:48, :] + recv[k, q, 0:16, :]
                    dy[k, pl.ds(pl.multiple_of(at, 16), 16), :] = first
                    dy[k, pl.ds(pl.multiple_of(at + 16, 16), 16), :] = recv[k, q, 16:32, :]
                    if s == 3:
                        dy[k, pl.ds(pl.multiple_of(at + 32, 16), 16), :] = recv[k, q, 32:48, :]
        for device in (to_x, to_yp, to_ym):
            push(L1, c, n, rep, 0, UNIT, device)
        push(LC1, c, n, rep, 0, UNIT, to_core)

    def stage2(c, n):
        wait_rows(rsem.at[L1, c], c, n, 3 * UNIT)
        push(L2, c, n, unit(0, -1), 0, A, to_yp)
        push(L2, c, n, unit(0, 1), A, BR, to_ym)
        push(L2, c, n, unit(0, 1), A, BR, to_x)
        push(L2, c, n, unit(1, 0), 0, A, to_yp)
        push(L2, c, n, unit(1, 0), 0, A, to_ym)
        push(L2, c, n, unit(0, -1), A, BR, to_x)
        for u in (unit(1, 0), unit(0, 1), unit(0, -1)):
            push(LC2, c, n, u, 0, UNIT, to_core)

    def stage3(c, n):
        wait_rows(rsem.at[L2, c], c, n, 3 * UNIT)
        push(L3, c, n, unit(1, -1), 0, A1, to_yp)
        push(L3, c, n, unit(1, 1), A1, A - A1, to_ym)
        push(L3, c, n, unit(0, 2), A, BR, to_x)
        for u in (unit(0, 2), unit(1, 1), unit(1, -1)):
            push(LC3, c, n, u, 0, UNIT, to_core)

    def stage4(c, n):
        wait_rows(rsem.at[L3, c], c, n, UNIT)
        push(LC4, c, n, unit(1, 2), 0, UNIT, to_core)

    def arrived(c, n):
        wait_rows(rsem.at[LC1, c], c, n, UNIT)
        wait_rows(rsem.at[LC2, c], c, n, 3 * UNIT)
        wait_rows(rsem.at[LC3, c], c, n, 3 * UNIT)

    def multiply(k, b):
        at = pl.ds(pl.multiple_of(b * BLK, BLK), BLK)
        rows = jnp.concatenate([dy[2 * k, at, :], dy[2 * k + 1, at, :]], axis=1)
        wc = wv[:, pl.ds(pl.multiple_of(k * 2 * LANES, 2 * LANES), 2 * LANES)]
        gacc[k % 2] += jnp.dot(ht[:, at], rows, preferred_element_type=jnp.float32)
        acc[at, :] += lax.dot_general(
            rows, wc, (((1,), (1,)), ((), ())), preferred_element_type=jnp.float32
        )

    def flush(b):
        def body(i, _):
            n = b * (BLK // GRP) + i
            d_out[0, group_rows(n), :] = acc[local_rows(n), :].astype(jnp.bfloat16)
            return 0

        lax.fori_loop(0, BLK // GRP, body, 0)

    late_block = (1 - lo) * 2 + (y + 2) % 4 // 2

    def completes(c):
        wide_c = (c >= HEAD) & (c < NC - TAIL)
        return (c >= 0) & (c < NC) & (wide_c | (tile0(c) % 2 == 1))

    def early(c):
        k = tile0(c) // 2
        gacc[k % 2] = jnp.zeros(gacc.shape[1:], jnp.float32)

        def body(i, _):
            if TAIL:

                @pl.when((c == NC - 1) & (i == 2))
                def _():
                    stage4(NC - 1, 1)

                @pl.when((c == NC - 3) & (i == 1))
                def _():
                    stage2(NC - 1, 1)

            b = (late_block + 1 + i) % 4
            multiply(k, b)

            @pl.when(k == PAIRS - 1)
            def _():
                flush(b)

            return 0

        lax.fori_loop(0, 3, body, 0)

    def late(c, n):
        if n == 1:
            wait_rows(rsem.at[LC4, c - 1], c - 1, 1, UNIT)
        wait_rows(rsem.at[LC4, c], c, n, UNIT)
        k = tile0(c) // 2
        multiply(k, late_block)
        cols = pl.ds(pl.multiple_of(k * 2 * LANES, 2 * LANES), 2 * LANES)
        gd_out[0, :, cols] = gacc[k % 2].astype(jnp.bfloat16)

        @pl.when(k == PAIRS - 1)
        def _():
            flush(late_block)

    def turn_hidden(part):
        def body(i, _):
            at = pl.ds(pl.multiple_of((part * 9 + i) * 128, 128), 128)
            ht[:, at] = hb[at, :].T
            return 0

        lax.fori_loop(0, 9, body, 0)
        at = pl.ds(pl.multiple_of(part * BLK, BLK), BLK)
        acc[at, :] = jnp.zeros((BLK, FFD), jnp.float32)

    load_g.wait()
    make_windows(0, 1)
    pl.semaphore_wait(bar, len(peers))
    send_windows(0, 1)
    lax.fori_loop(0, 32, start_hidden, 0)
    load_w.start()
    prep(1, 1)
    make_windows(2, 2)

    def step(t, _):
        def stage(lag, fn, but=0):
            c = t - lag

            @pl.when((c >= 0) & (c < NC - but))
            def _():
                wide(c, fn)

        stage(0, stage1)

        @pl.when(t == 0)
        def _():
            send_windows(2, 2)


        @pl.when((t > 0) & (t + 2 < NC))
        def _():
            wide(t + 2, prep)

        stage(1, stage2, 1)

        @pl.when(completes(t - 4) & (t < NC))
        def _():
            wide(t - 4, late)

        stage(2, stage3)
        stage(3, stage4, 1)

        @pl.when(completes(t - 4) & (t >= NC))
        def _():
            wide(t - 4, late)

        @pl.when(t == 0)
        def _():
            pltpu.make_async_copy(hb, hb, lsem.at[2]).wait()
            load_w.wait()

        @pl.when(t < 4)
        def _():
            turn_hidden(t)

        stage(2, arrived)

        @pl.when(completes(t - 2))
        def _():
            early(t - 2)

        return 0

    lax.fori_loop(0, NC + 4, step, 0)

    def drain(c, _):
        def one(c, n):
            wait_windows(ssem.at[0, c], c, n)
            wait_rows(ssem.at[1, c], c, n, 15 * UNIT)

        wide(c, one)
        return 0

    lax.fori_loop(0, NC, drain, 0)


def store_kernel(d_in, gd_in, d_hbm, gd_hbm, sem):
    d = pltpu.make_async_copy(d_in, d_hbm, sem.at[0])
    g = pltpu.make_async_copy(gd_in, gd_hbm, sem.at[1])
    d.start()
    g.start()
    d.wait()
    g.wait()


def per_device(grad_out, routes, probs, rows_hidden, w_down):
    bf = jnp.bfloat16
    any_spec = pl.BlockSpec(memory_space=pl.ANY)
    vmem = pl.BlockSpec(memory_space=pltpu.VMEM)
    d_shape, gd_shape = (1, ROWS, FFD), (1, FFD, D)
    d_rows, grad = pl.pallas_call(
        gather_kernel,
        out_shape=(pltpu.VMEM(d_shape, bf), pltpu.VMEM(gd_shape, bf)),
        in_specs=[any_spec] * 5,
        out_specs=(vmem, vmem),
        scratch_shapes=[
            pltpu.VMEM((2, TOK), jnp.int32),
            pltpu.VMEM((2, TOK), jnp.float32),
            pltpu.VMEM((COLS, ROWS, LANES), bf),
            pltpu.VMEM((COLS, EXPERTS * WIN, LANES), bf),
            pltpu.VMEM((COLS, 8, WIN, LANES), bf),
            pltpu.VMEM((FFD, ROWS), bf),
            pltpu.VMEM((FFD, D), bf),
            pltpu.VMEM((TOK, D), bf),
            pltpu.VMEM((ROWS, FFD), jnp.float32),
            pltpu.VMEM((2, FFD, 2 * LANES), jnp.float32),
            pltpu.VMEM((EXPERTS * WIN, TOK), bf),
            pltpu.VMEM((EXPERTS * WIN, LANES), jnp.float32),
            pltpu.SemaphoreType.DMA((2, NC)),
            pltpu.SemaphoreType.DMA((8, NC)),
            pltpu.SemaphoreType.DMA((5,)),
        ],
        compiler_params=pltpu.CompilerParams(
            collective_id=0, has_side_effects=True, vmem_limit_bytes=54 * 2**20
        ),
        cost_estimate=pl.CostEstimate(
            flops=4 * ROWS * D * FFD, bytes_accessed=2 * (2 * ROWS * FFD + 2 * FFD * D), transcendentals=0
        ),
    )(routes.T, probs.T, grad_out, rows_hidden, w_down)
    return pl.pallas_call(
        store_kernel,
        out_shape=(jax.ShapeDtypeStruct(d_shape, bf), jax.ShapeDtypeStruct(gd_shape, bf)),
        in_specs=[vmem, vmem],
        out_specs=(any_spec, any_spec),
        scratch_shapes=[pltpu.SemaphoreType.DMA((2,))],
        compiler_params=pltpu.CompilerParams(vmem_limit_bytes=2 * 2**20),
    )(
        pltpu.with_memory_space_constraint(d_rows, pltpu.VMEM),
        pltpu.with_memory_space_constraint(grad, pltpu.VMEM),
    )


def solution(mesh):
    return jax.shard_map(
        per_device,
        mesh=mesh,
        in_specs=(
            P(("rep", "exp"), None),
            P(("rep", "exp"), None),
            P(("rep", "exp"), None),
            P("exp", None, "rep"),
            P("exp", "rep", None),
        ),
        out_specs=(P("exp", None, "rep"), P("exp", "rep", None)),
        check_vma=False,
    )
```

```python
import jax
import jax.numpy as jnp
from jax import lax
from jax.experimental import pallas as pl
from jax.experimental.pallas import tpu as pltpu
from jax.sharding import PartitionSpec as P

CAP = 36
EXPERTS = 8
TOK = 128
D = 3072
FFD = 512
ROWS = 4608
LANES = 128
COLS = D // LANES
PAIRS = COLS // 2
HEAD, TAIL = 2, 2
NC = HEAD + (COLS - HEAD - TAIL) // 2 + TAIL
WIN = 48
GRP = 4 * CAP
UNIT = 2 * GRP
NU = 16
A = 160
A1 = 64
BR = UNIT - A
MESH = pl.DeviceIdType.MESH

LEXP, L1, L2, L3, LC1, LC2, LC3, LC4 = range(8)
BLK = 4 * UNIT
DONE = 2


def group_rows(hi, i):
    u, part = i // 2, i % 2
    g = (u + 8 * part) % 16 * 2 + (hi + part) % 2
    return pl.ds(pl.multiple_of(g * GRP, 16), GRP)


def local_rows(i):
    return pl.ds(pl.multiple_of(i * GRP, 16), GRP)


def block_rows(b):
    return pl.ds(pl.multiple_of(b * BLK, BLK), BLK)


def late_block(lo, y):
    return (1 - lo) * 2 + (y + 2) % 4 // 2


def gather_kernel(
    rt_hbm, pt_hbm, g_hbm, h_hbm, w_hbm, rows_out, acc, gacc, grad, ht, wv,
    rt_ref, pt_ref, dy, send, recv, hb, gv, sel, prow,
    ssem, rsem, lsem,
):
    rep = lax.axis_index("rep")
    ex = lax.axis_index("exp")
    lo, y, core = rep // 8, (rep // 2) % 4, rep % 2
    hi, z = ex // 4, ex % 4

    def unit(dl, dyy):
        return ((lo + dl) % 2 * 4 + (y + dyy + 4) % 4) * 2 + core

    to_x = (unit(1, 0), ex)
    to_yp = (unit(0, 1), ex)
    to_ym = (unit(0, -1), ex)
    to_core = ((lo * 4 + y) * 2 + 1 - core, ex)
    spread = []
    for dh in (1, 0):
        for dz in (2, 1, 3, 0):
            if dh or dz:
                hz = (hi + dh) % 2 * 4 + (z + dz) % 4
                spread.append((dh, (unit(dh, 0), hz), hz))
    peers = [to_x, to_yp, to_ym, to_core] + [s[1] for s in spread]

    load_g = pltpu.make_async_copy(g_hbm, gv, lsem.at[0])
    load_w = pltpu.make_async_copy(w_hbm.at[0], wv, lsem.at[1])
    load_r = pltpu.make_async_copy(rt_hbm, rt_ref, lsem.at[3])
    load_p = pltpu.make_async_copy(pt_hbm, pt_ref, lsem.at[4])
    load_r.start()
    load_p.start()
    load_g.start()

    bar = pltpu.get_barrier_semaphore()
    for p in peers:
        pl.semaphore_signal(bar, inc=1, device_id=p, device_id_type=MESH)

    def start_hidden(i, _):
        pltpu.make_async_copy(
            h_hbm.at[0, group_rows(hi, i)], hb.at[local_rows(i)], lsem.at[2]
        ).start()
        return 0

    load_r.wait()
    load_p.wait()
    rt = rt_ref[...]
    pt = pt_ref[...]
    erow = lax.broadcasted_iota(jnp.int32, (EXPERTS, TOK), 0)
    oh0 = (rt[0:1] == erow).astype(jnp.float32)
    oh1 = (rt[1:2] == erow).astype(jnp.float32)
    upper = (
        lax.broadcasted_iota(jnp.int32, (TOK, TOK), 0)
        < lax.broadcasted_iota(jnp.int32, (TOK, TOK), 1)
    ).astype(jnp.float32)
    before = jnp.dot(oh0 + oh1, upper, preferred_element_type=jnp.float32)
    slot0 = jnp.sum(oh0 * before, axis=0, keepdims=True).astype(jnp.int32)
    slot1 = jnp.sum(oh1 * before, axis=0, keepdims=True).astype(jnp.int32)
    t0 = rt[0:1] * WIN + slot0 + 4 * z
    t1 = rt[1:2] * WIN + slot1 + 4 * z
    row = lax.broadcasted_iota(jnp.int32, (EXPERTS * WIN, TOK), 0)
    m0 = row == t0
    m1 = row == t1
    sel[...] = (m0 | m1).astype(jnp.float32).astype(jnp.bfloat16)
    pw = jnp.where(m0, pt[0:1], 0.0) + jnp.where(m1, pt[1:2], 0.0)
    prow[...] = jnp.broadcast_to(jnp.sum(pw, axis=1, keepdims=True), prow.shape)

    def tile0(c):
        return jnp.where(c < HEAD, c, jnp.where(c < NC - TAIL, 2 * c - HEAD, c + COLS - NC))

    def wide(c, fn):
        one = (c < HEAD) | (c >= NC - TAIL)

        @pl.when(one)
        def _():
            fn(c, 1)

        @pl.when(jnp.logical_not(one))
        def _():
            fn(c, 2)

    def remote(src, dst, stage, c, device):
        s = 0 if stage == LEXP else 1
        pltpu.make_async_remote_copy(
            src_ref=src, dst_ref=dst, send_sem=ssem.at[s, c], recv_sem=rsem.at[stage, c],
            device_id=device, device_id_type=MESH,
        ).start()

    def wait_rows(sem, c, n, rows):
        ref = dy.at[pl.ds(tile0(c), n), pl.ds(0, rows)]
        pltpu.make_async_copy(ref, ref, sem).wait()

    def wait_windows(sem, c, n):
        ref = recv.at[pl.ds(tile0(c), n), pl.ds(0, 7)]
        pltpu.make_async_copy(ref, ref, sem).wait()

    def push(stage, c, n, u, start, rows, device):
        ref = dy.at[pl.ds(tile0(c), n), pl.ds(pl.multiple_of(u * UNIT + start, 16), rows)]
        remote(ref, ref, stage, c, device)

    def make_windows(c, n):
        g = gv[:, pl.ds(pl.multiple_of(tile0(c) * LANES, LANES), n * LANES)]
        rows = jnp.dot(sel[...], g, preferred_element_type=jnp.float32)
        for i in range(n):
            tile = rows[:, i * LANES : (i + 1) * LANES] * prow[...]
            send[tile0(c) + i] = tile.astype(jnp.bfloat16)

    def send_windows(c, n):
        for dh, device, e in spread:
            remote(
                send.at[pl.ds(tile0(c), n), pl.ds(pl.multiple_of(e * WIN, 16), WIN)],
                recv.at[pl.ds(tile0(c), n), dh * 4 + z],
                LEXP, c, device,
            )
        for i in range(n):
            recv[tile0(c) + i, z] = send[tile0(c) + i, pl.ds(pl.multiple_of(ex * WIN, 16), WIN), :]

    def prep(c, n):
        make_windows(c, n)
        send_windows(c, n)

    def stage1(c, n):
        wait_windows(rsem.at[LEXP, c], c, n)
        for i in range(n):
            k = tile0(c) + i
            for part in range(2):
                for s in range(4):
                    at = rep * UNIT + part * GRP + s * 32
                    q = part * 4 + s
                    if s == 0:
                        first = recv[k, q, 0:16, :]
                    else:
                        first = recv[k, q - 1, 32:48, :] + recv[k, q, 0:16, :]
                    dy[k, pl.ds(pl.multiple_of(at, 16), 16), :] = first
                    dy[k, pl.ds(pl.multiple_of(at + 16, 16), 16), :] = recv[k, q, 16:32, :]
                    if s == 3:
                        dy[k, pl.ds(pl.multiple_of(at + 32, 16), 16), :] = recv[k, q, 32:48, :]
        for device in (to_x, to_yp, to_ym):
            push(L1, c, n, rep, 0, UNIT, device)
        push(LC1, c, n, rep, 0, UNIT, to_core)

    def stage2(c, n):
        wait_rows(rsem.at[L1, c], c, n, 3 * UNIT)
        push(L2, c, n, unit(0, -1), 0, A, to_yp)
        push(L2, c, n, unit(0, 1), A, BR, to_ym)
        push(L2, c, n, unit(0, 1), A, BR, to_x)
        push(L2, c, n, unit(1, 0), 0, A, to_yp)
        push(L2, c, n, unit(1, 0), 0, A, to_ym)
        push(L2, c, n, unit(0, -1), A, BR, to_x)
        for u in (unit(1, 0), unit(0, 1), unit(0, -1)):
            push(LC2, c, n, u, 0, UNIT, to_core)

    def stage3(c, n):
        wait_rows(rsem.at[L2, c], c, n, 3 * UNIT)
        push(L3, c, n, unit(1, -1), 0, A1, to_yp)
        push(L3, c, n, unit(1, 1), A1, A - A1, to_ym)
        push(L3, c, n, unit(0, 2), A, BR, to_x)
        for u in (unit(0, 2), unit(1, 1), unit(1, -1)):
            push(LC3, c, n, u, 0, UNIT, to_core)

    def stage4(c, n):
        wait_rows(rsem.at[L3, c], c, n, UNIT)
        push(LC4, c, n, unit(1, 2), 0, UNIT, to_core)

    def arrived(c, n):
        wait_rows(rsem.at[LC1, c], c, n, UNIT)
        wait_rows(rsem.at[LC2, c], c, n, 3 * UNIT)
        wait_rows(rsem.at[LC3, c], c, n, 3 * UNIT)

    def multiply(k, b):
        at = pl.ds(pl.multiple_of(b * BLK, BLK), BLK)
        rows = jnp.concatenate([dy[2 * k, at, :], dy[2 * k + 1, at, :]], axis=1)
        wc = wv[:, pl.ds(pl.multiple_of(k * 2 * LANES, 2 * LANES), 2 * LANES)]
        gacc[k % 2] += jnp.dot(ht[:, at], rows, preferred_element_type=jnp.float32)
        acc[at, :] += lax.dot_general(
            rows, wc, (((1,), (1,)), ((), ())), preferred_element_type=jnp.float32
        )

    late = late_block(lo, y)

    def completes(c):
        wide_c = (c >= HEAD) & (c < NC - TAIL)
        return (c >= 0) & (c < NC) & (wide_c | (tile0(c) % 2 == 1))

    def early(c):
        k = tile0(c) // 2
        gacc[k % 2] = jnp.zeros(gacc.shape[1:], jnp.float32)

        def body(i, _):
            @pl.when((c == NC - 3) & (i == 1))
            def _():
                stage2(NC - 1, 1)

            multiply(k, (late + 1 + i) % 4)
            return 0

        lax.fori_loop(0, jnp.where(c == NC - 1, DONE, 3), body, 0)

    def finish(c, n):
        if n == 1:
            wait_rows(rsem.at[LC4, c - 1], c - 1, 1, UNIT)
        wait_rows(rsem.at[LC4, c], c, n, UNIT)
        k = tile0(c) // 2
        multiply(k, late)
        cols = pl.ds(pl.multiple_of(k * 2 * LANES, 2 * LANES), 2 * LANES)
        grad[:, cols] = gacc[k % 2].astype(jnp.bfloat16)

    def turn_hidden(part):
        def body(i, _):
            at = pl.ds(pl.multiple_of((part * 9 + i) * 128, 128), 128)
            ht[:, at] = hb[at, :].T
            return 0

        lax.fori_loop(0, 9, body, 0)
        at = pl.ds(pl.multiple_of(part * BLK, BLK), BLK)
        acc[at, :] = jnp.zeros((BLK, FFD), jnp.float32)

    load_g.wait()
    make_windows(0, 1)
    pl.semaphore_wait(bar, len(peers))
    send_windows(0, 1)
    lax.fori_loop(0, 32, start_hidden, 0)
    load_w.start()
    prep(1, 1)
    make_windows(2, 2)

    def step(t, _):
        def stage(lag, fn, but=0):
            c = t - lag

            @pl.when((c >= 0) & (c < NC - but))
            def _():
                wide(c, fn)

        stage(0, stage1)

        @pl.when(t == 0)
        def _():
            send_windows(2, 2)


        @pl.when((t > 0) & (t + 2 < NC))
        def _():
            wide(t + 2, prep)

        stage(1, stage2, 1)

        @pl.when(completes(t - 4) & (t < NC))
        def _():
            wide(t - 4, finish)

        stage(2, stage3)
        @pl.when(completes(t - 4) & (t >= NC))
        def _():
            wide(t - 4, finish)

        stage(3, stage4, 1)

        @pl.when(t == 0)
        def _():
            pltpu.make_async_copy(hb, hb, lsem.at[2]).wait()
            load_w.wait()

        @pl.when(t < 4)
        def _():
            turn_hidden(t)

        stage(2, arrived)

        @pl.when(completes(t - 2))
        def _():
            early(t - 2)

        return 0

    lax.fori_loop(0, NC + 2, step, 0)
    stage4(NC - 1, 1)
    for i in range(DONE, 4):
        if i == 3:
            for c in (NC - 2, NC - 1):
                wait_rows(rsem.at[LC4, c], c, 1, UNIT)
        at = block_rows((late + 1 + i) % 4)
        for k in range(2):
            rows_out[(i - DONE) * BLK : (i - DONE + 1) * BLK, k * LANES : (k + 1) * LANES] = dy[
                COLS - 2 + k, at, :
            ]

    def drain(c, _):
        def one(c, n):
            wait_windows(ssem.at[0, c], c, n)
            wait_rows(ssem.at[1, c], c, n, 15 * UNIT)

        wide(c, one)
        return 0

    lax.fori_loop(0, NC, drain, 0)


def store_kernel(rows_in, acc, gacc, grad, ht, wv, d_hbm, gd_hbm, d_buf, g_buf, g_sum, sem):
    rep, ex = lax.axis_index("rep"), lax.axis_index("exp")
    late, hi = late_block(rep // 8, (rep // 2) % 4), ex // 4
    last = (PAIRS - 1) * 2 * LANES
    first = pltpu.make_async_copy(grad.at[:, pl.ds(0, last)], gd_hbm.at[0, :, pl.ds(0, last)], sem.at[0])
    first.start()
    g_sum[...] = gacc[(PAIRS - 1) % 2]

    def body(i, _):
        b = (late + 1 + i) % 4
        at = block_rows(b)

        @pl.when(i < DONE)
        def _():
            d_buf[at, :] = acc[at, :].astype(jnp.bfloat16)

        @pl.when(i >= DONE)
        def _():
            rows = rows_in[block_rows(i - DONE), :]
            part = lax.dot_general(
                rows, wv[:, last:], (((1,), (1,)), ((), ())), preferred_element_type=jnp.float32
            )
            d_buf[at, :] = (acc[at, :] + part).astype(jnp.bfloat16)
            g_sum[...] += jnp.dot(ht[:, at], rows, preferred_element_type=jnp.float32)

        def put(k, _):
            n = b * (BLK // GRP) + k
            pltpu.make_async_copy(
                d_buf.at[local_rows(n)], d_hbm.at[0, group_rows(hi, n)], sem.at[1]
            ).start()
            return 0

        lax.fori_loop(0, BLK // GRP, put, 0)
        return 0

    lax.fori_loop(0, 4, body, 0)
    g_buf[...] = g_sum[...].astype(jnp.bfloat16)
    second = pltpu.make_async_copy(g_buf, gd_hbm.at[0, :, pl.ds(last, 2 * LANES)], sem.at[2])
    second.start()
    first.wait()
    pltpu.make_async_copy(d_buf, d_hbm.at[0], sem.at[1]).wait()
    second.wait()


def per_device(grad_out, routes, probs, rows_hidden, w_down):
    bf = jnp.bfloat16
    any_spec = pl.BlockSpec(memory_space=pl.ANY)
    vmem = pl.BlockSpec(memory_space=pltpu.VMEM)
    kept = pl.pallas_call(
        gather_kernel,
        out_shape=(
            pltpu.VMEM(((4 - DONE) * BLK, 2 * LANES), bf),
            pltpu.VMEM((ROWS, FFD), jnp.float32),
            pltpu.VMEM((2, FFD, 2 * LANES), jnp.float32),
            pltpu.VMEM((FFD, D), bf),
            pltpu.VMEM((FFD, ROWS), bf),
            pltpu.VMEM((FFD, D), bf),
        ),
        in_specs=[any_spec] * 5,
        out_specs=[vmem] * 6,
        scratch_shapes=[
            pltpu.VMEM((2, TOK), jnp.int32),
            pltpu.VMEM((2, TOK), jnp.float32),
            pltpu.VMEM((COLS, ROWS, LANES), bf),
            pltpu.VMEM((COLS, EXPERTS * WIN, LANES), bf),
            pltpu.VMEM((COLS, 8, WIN, LANES), bf),
            pltpu.VMEM((ROWS, FFD), bf),
            pltpu.VMEM((TOK, D), bf),
            pltpu.VMEM((EXPERTS * WIN, TOK), bf),
            pltpu.VMEM((EXPERTS * WIN, LANES), jnp.float32),
            pltpu.SemaphoreType.DMA((2, NC)),
            pltpu.SemaphoreType.DMA((8, NC)),
            pltpu.SemaphoreType.DMA((5,)),
        ],
        compiler_params=pltpu.CompilerParams(
            collective_id=0, has_side_effects=True, vmem_limit_bytes=41 * 2**20
        ),
        cost_estimate=pl.CostEstimate(
            flops=4 * ROWS * D * FFD, bytes_accessed=2 * (2 * ROWS * FFD + 2 * FFD * D), transcendentals=0
        ),
    )(routes.T, probs.T, grad_out, rows_hidden, w_down)
    return pl.pallas_call(
        store_kernel,
        out_shape=(
            jax.ShapeDtypeStruct((1, ROWS, FFD), bf),
            jax.ShapeDtypeStruct((1, FFD, D), bf),
        ),
        in_specs=[vmem] * 6,
        out_specs=(any_spec, any_spec),
        scratch_shapes=[
            pltpu.VMEM((ROWS, FFD), bf),
            pltpu.VMEM((FFD, 2 * LANES), bf),
            pltpu.VMEM((FFD, 2 * LANES), jnp.float32),
            pltpu.SemaphoreType.DMA((3,)),
        ],
        compiler_params=pltpu.CompilerParams(vmem_limit_bytes=10 * 2**20),
    )(*(pltpu.with_memory_space_constraint(a, pltpu.VMEM) for a in kept))


def solution(mesh):
    return jax.shard_map(
        per_device,
        mesh=mesh,
        in_specs=(
            P(("rep", "exp"), None),
            P(("rep", "exp"), None),
            P(("rep", "exp"), None),
            P("exp", None, "rep"),
            P("exp", "rep", None),
        ),
        out_specs=(P("exp", None, "rep"), P("exp", "rep", None)),
        check_vma=False,
    )
```

```python
import jax
import jax.numpy as jnp
from jax import lax
from jax.experimental import pallas as pl
from jax.experimental.pallas import tpu as pltpu
from jax.sharding import PartitionSpec as P

CAP = 36
EXPERTS = 8
TOK = 128
D = 3072
FFD = 512
ROWS = 4608
LANES = 128
COLS = D // LANES
PAIRS = COLS // 2
HEAD, TAIL = 2, 2
NC = HEAD + (COLS - HEAD - TAIL) // 2 + TAIL
WIN = 48
GRP = 4 * CAP
UNIT = 2 * GRP
NU = 16
A = 160
A1 = 64
BR = UNIT - A
MESH = pl.DeviceIdType.MESH

LEXP, L1, L2, L3, LC1, LC2, LC3, LC4 = range(8)
BLK = 4 * UNIT
DONE = 2


def group_rows(hi, i):
    u, part = i // 2, i % 2
    g = (u + 8 * part) % 16 * 2 + (hi + part) % 2
    return pl.ds(pl.multiple_of(g * GRP, 16), GRP)


def local_rows(i):
    return pl.ds(pl.multiple_of(i * GRP, 16), GRP)


def block_rows(b):
    return pl.ds(pl.multiple_of(b * BLK, BLK), BLK)


def late_block(lo, y):
    return (1 - lo) * 2 + (y + 2) % 4 // 2


def gather_kernel(
    rt_hbm, pt_hbm, g_hbm, h_hbm, w_hbm, rows_out, acc, gacc, grad, ht, wv,
    rt_ref, pt_ref, dy, send, recv, hb, gv, sel, prow,
    ssem, rsem, lsem,
):
    rep = lax.axis_index("rep")
    ex = lax.axis_index("exp")
    lo, y, core = rep // 8, (rep // 2) % 4, rep % 2
    hi, z = ex // 4, ex % 4

    def unit(dl, dyy):
        return ((lo + dl) % 2 * 4 + (y + dyy + 4) % 4) * 2 + core

    to_x = (unit(1, 0), ex)
    to_yp = (unit(0, 1), ex)
    to_ym = (unit(0, -1), ex)
    to_core = ((lo * 4 + y) * 2 + 1 - core, ex)
    spread = []
    for dh in (1, 0):
        for dz in (2, 1, 3, 0):
            if dh or dz:
                hz = (hi + dh) % 2 * 4 + (z + dz) % 4
                spread.append((dh, (unit(dh, 0), hz), hz))
    peers = [to_x, to_yp, to_ym, to_core] + [s[1] for s in spread]

    load_g = pltpu.make_async_copy(g_hbm, gv, lsem.at[0])
    load_w = pltpu.make_async_copy(w_hbm.at[0], wv, lsem.at[1])
    load_r = pltpu.make_async_copy(rt_hbm, rt_ref, lsem.at[3])
    load_p = pltpu.make_async_copy(pt_hbm, pt_ref, lsem.at[4])
    load_r.start()
    load_p.start()
    load_g.start()

    bar = pltpu.get_barrier_semaphore()
    for p in peers:
        pl.semaphore_signal(bar, inc=1, device_id=p, device_id_type=MESH)

    def start_hidden(i, _):
        pltpu.make_async_copy(
            h_hbm.at[0, group_rows(hi, i)], hb.at[local_rows(i)], lsem.at[2]
        ).start()
        return 0

    load_r.wait()
    load_p.wait()
    rt = rt_ref[...]
    pt = pt_ref[...]
    erow = lax.broadcasted_iota(jnp.int32, (EXPERTS, TOK), 0)
    oh0 = (rt[0:1] == erow).astype(jnp.float32)
    oh1 = (rt[1:2] == erow).astype(jnp.float32)
    upper = (
        lax.broadcasted_iota(jnp.int32, (TOK, TOK), 0)
        < lax.broadcasted_iota(jnp.int32, (TOK, TOK), 1)
    ).astype(jnp.float32)
    before = jnp.dot(oh0 + oh1, upper, preferred_element_type=jnp.float32)
    slot0 = jnp.sum(oh0 * before, axis=0, keepdims=True).astype(jnp.int32)
    slot1 = jnp.sum(oh1 * before, axis=0, keepdims=True).astype(jnp.int32)
    t0 = rt[0:1] * WIN + slot0 + 4 * z
    t1 = rt[1:2] * WIN + slot1 + 4 * z
    row = lax.broadcasted_iota(jnp.int32, (EXPERTS * WIN, TOK), 0)
    m0 = row == t0
    m1 = row == t1
    sel[...] = (m0 | m1).astype(jnp.float32).astype(jnp.bfloat16)
    pw = jnp.where(m0, pt[0:1], 0.0) + jnp.where(m1, pt[1:2], 0.0)
    prow[...] = jnp.broadcast_to(jnp.sum(pw, axis=1, keepdims=True), prow.shape)

    def tile0(c):
        return jnp.where(c < HEAD, c, jnp.where(c < NC - TAIL, 2 * c - HEAD, c + COLS - NC))

    def wide(c, fn):
        one = (c < HEAD) | (c >= NC - TAIL)

        @pl.when(one)
        def _():
            fn(c, 1)

        @pl.when(jnp.logical_not(one))
        def _():
            fn(c, 2)

    def remote(src, dst, stage, c, device):
        s = 0 if stage == LEXP else 1
        pltpu.make_async_remote_copy(
            src_ref=src, dst_ref=dst, send_sem=ssem.at[s, c], recv_sem=rsem.at[stage, c],
            device_id=device, device_id_type=MESH,
        ).start()

    def wait_rows(sem, c, n, rows):
        ref = dy.at[pl.ds(tile0(c), n), pl.ds(0, rows)]
        pltpu.make_async_copy(ref, ref, sem).wait()

    def wait_windows(sem, c, n):
        ref = recv.at[pl.ds(tile0(c), n), pl.ds(0, 7)]
        pltpu.make_async_copy(ref, ref, sem).wait()

    def push(stage, c, n, u, start, rows, device):
        ref = dy.at[pl.ds(tile0(c), n), pl.ds(pl.multiple_of(u * UNIT + start, 16), rows)]
        remote(ref, ref, stage, c, device)

    def make_windows(c, n):
        g = gv[:, pl.ds(pl.multiple_of(tile0(c) * LANES, LANES), n * LANES)]
        rows = jnp.dot(sel[...], g, preferred_element_type=jnp.float32)
        for i in range(n):
            tile = rows[:, i * LANES : (i + 1) * LANES] * prow[...]
            send[tile0(c) + i] = tile.astype(jnp.bfloat16)

    def send_windows(c, n):
        for dh, device, e in spread:
            remote(
                send.at[pl.ds(tile0(c), n), pl.ds(pl.multiple_of(e * WIN, 16), WIN)],
                recv.at[pl.ds(tile0(c), n), dh * 4 + z],
                LEXP, c, device,
            )
        for i in range(n):
            recv[tile0(c) + i, z] = send[tile0(c) + i, pl.ds(pl.multiple_of(ex * WIN, 16), WIN), :]

    def prep(c, n):
        make_windows(c, n)
        send_windows(c, n)

    def stage1(c, n):
        wait_windows(rsem.at[LEXP, c], c, n)
        for i in range(n):
            k = tile0(c) + i
            for part in range(2):
                for s in range(4):
                    at = rep * UNIT + part * GRP + s * 32
                    q = part * 4 + s
                    if s == 0:
                        first = recv[k, q, 0:16, :]
                    else:
                        first = recv[k, q - 1, 32:48, :] + recv[k, q, 0:16, :]
                    dy[k, pl.ds(pl.multiple_of(at, 16), 16), :] = first
                    dy[k, pl.ds(pl.multiple_of(at + 16, 16), 16), :] = recv[k, q, 16:32, :]
                    if s == 3:
                        dy[k, pl.ds(pl.multiple_of(at + 32, 16), 16), :] = recv[k, q, 32:48, :]
        for device in (to_x, to_yp, to_ym):
            push(L1, c, n, rep, 0, UNIT, device)
        push(LC1, c, n, rep, 0, UNIT, to_core)

    def stage2(c, n):
        wait_rows(rsem.at[L1, c], c, n, 3 * UNIT)
        push(L2, c, n, unit(0, -1), 0, A, to_yp)
        push(L2, c, n, unit(0, 1), A, BR, to_ym)
        push(L2, c, n, unit(0, 1), A, BR, to_x)
        push(L2, c, n, unit(1, 0), 0, A, to_yp)
        push(L2, c, n, unit(1, 0), 0, A, to_ym)
        push(L2, c, n, unit(0, -1), A, BR, to_x)
        for u in (unit(1, 0), unit(0, 1), unit(0, -1)):
            push(LC2, c, n, u, 0, UNIT, to_core)

    def stage3(c, n):
        wait_rows(rsem.at[L2, c], c, n, 3 * UNIT)
        push(L3, c, n, unit(1, -1), 0, A1, to_yp)
        push(L3, c, n, unit(1, 1), A1, A - A1, to_ym)
        push(L3, c, n, unit(0, 2), A, BR, to_x)
        for u in (unit(0, 2), unit(1, 1), unit(1, -1)):
            push(LC3, c, n, u, 0, UNIT, to_core)

    def stage4(c, n):
        wait_rows(rsem.at[L3, c], c, n, UNIT)
        push(LC4, c, n, unit(1, 2), 0, UNIT, to_core)

    def arrived(c, n):
        wait_rows(rsem.at[LC1, c], c, n, UNIT)
        wait_rows(rsem.at[LC2, c], c, n, 3 * UNIT)
        wait_rows(rsem.at[LC3, c], c, n, 3 * UNIT)

    def multiply(k, b):
        at = pl.ds(pl.multiple_of(b * BLK, BLK), BLK)
        rows = jnp.concatenate([dy[2 * k, at, :], dy[2 * k + 1, at, :]], axis=1)
        wc = wv[:, pl.ds(pl.multiple_of(k * 2 * LANES, 2 * LANES), 2 * LANES)]
        gacc[k % 2] += jnp.dot(ht[:, at], rows, preferred_element_type=jnp.float32)
        acc[at, :] += lax.dot_general(
            rows, wc, (((1,), (1,)), ((), ())), preferred_element_type=jnp.float32
        )

    late = late_block(lo, y)

    def completes(c):
        wide_c = (c >= HEAD) & (c < NC - TAIL)
        return (c >= 0) & (c < NC) & (wide_c | (tile0(c) % 2 == 1))

    def early(c):
        k = tile0(c) // 2
        gacc[k % 2] = jnp.zeros(gacc.shape[1:], jnp.float32)

        def body(i, _):
            @pl.when((c == NC - 3) & (i == 0))
            def _():
                stage2(NC - 1, 1)

            @pl.when((c == NC - 1) & (i == 1))
            def _():
                stage4(NC - 1, 1)

            multiply(k, (late + 1 + i) % 4)
            return 0

        lax.fori_loop(0, jnp.where(c == NC - 1, DONE, 3), body, 0)

    def finish(c, n):
        if n == 1:
            wait_rows(rsem.at[LC4, c - 1], c - 1, 1, UNIT)
        wait_rows(rsem.at[LC4, c], c, n, UNIT)
        k = tile0(c) // 2
        multiply(k, late)
        cols = pl.ds(pl.multiple_of(k * 2 * LANES, 2 * LANES), 2 * LANES)
        grad[:, cols] = gacc[k % 2].astype(jnp.bfloat16)

    def turn_hidden(part):
        def body(i, _):
            at = pl.ds(pl.multiple_of((part * 9 + i) * 128, 128), 128)
            ht[:, at] = hb[at, :].T
            return 0

        lax.fori_loop(0, 9, body, 0)

    load_g.wait()
    make_windows(0, 1)
    pl.semaphore_wait(bar, len(peers))
    send_windows(0, 1)
    lax.fori_loop(0, 32, start_hidden, 0)
    load_w.start()
    make_windows(1, 1)

    def clear(i, _):
        acc[block_rows(i), :] = jnp.zeros((BLK, FFD), jnp.float32)
        return 0

    lax.fori_loop(0, 4, clear, 0)
    send_windows(1, 1)
    make_windows(2, 2)

    def step(t, _):
        def stage(lag, fn, but=0):
            c = t - lag

            @pl.when((c >= 0) & (c < NC - but))
            def _():
                wide(c, fn)

        stage(0, stage1, 1)

        @pl.when(t == 0)
        def _():
            send_windows(2, 2)


        @pl.when((t > 0) & (t + 2 < NC))
        def _():
            wide(t + 2, prep)

        stage(1, stage2, 1)

        @pl.when(completes(t - 4) & (t < NC))
        def _():
            wide(t - 4, finish)

        stage(2, stage3)
        @pl.when(completes(t - 4) & (t >= NC))
        def _():
            wide(t - 4, finish)

        stage(3, stage4, 1)

        @pl.when(t == NC - 2)
        def _():
            stage1(NC - 1, 1)

        @pl.when(t == 0)
        def _():
            pltpu.make_async_copy(hb, hb, lsem.at[2]).wait()
            load_w.wait()

        @pl.when(t < 4)
        def _():
            turn_hidden(t)

        stage(2, arrived)

        @pl.when(completes(t - 2))
        def _():
            early(t - 2)

        return 0

    lax.fori_loop(0, NC + 2, step, 0)
    for i in range(DONE, 4):
        if i == 3:
            for c in (NC - 2, NC - 1):
                wait_rows(rsem.at[LC4, c], c, 1, UNIT)
        at = block_rows((late + 1 + i) % 4)
        for k in range(2):
            rows_out[(i - DONE) * BLK : (i - DONE + 1) * BLK, k * LANES : (k + 1) * LANES] = dy[
                COLS - 2 + k, at, :
            ]

    def drain(c, _):
        def one(c, n):
            wait_windows(ssem.at[0, c], c, n)
            wait_rows(ssem.at[1, c], c, n, 15 * UNIT)

        wide(c, one)
        return 0

    lax.fori_loop(0, NC, drain, 0)


def store_kernel(rows_in, acc, gacc, grad, ht, wv, d_hbm, gd_hbm, d_buf, g_buf, g_sum, sem):
    rep, ex = lax.axis_index("rep"), lax.axis_index("exp")
    late, hi = late_block(rep // 8, (rep // 2) % 4), ex // 4
    last = (PAIRS - 1) * 2 * LANES
    first = pltpu.make_async_copy(grad.at[:, pl.ds(0, last)], gd_hbm.at[0, :, pl.ds(0, last)], sem.at[0])
    first.start()
    g_sum[...] = gacc[(PAIRS - 1) % 2]

    def body(i, _):
        b = (late + 1 + i) % 4
        at = block_rows(b)

        @pl.when(i < DONE)
        def _():
            d_buf[at, :] = acc[at, :].astype(jnp.bfloat16)

        @pl.when(i >= DONE)
        def _():
            rows = rows_in[block_rows(i - DONE), :]
            part = lax.dot_general(
                rows, wv[:, last:], (((1,), (1,)), ((), ())), preferred_element_type=jnp.float32
            )
            d_buf[at, :] = (acc[at, :] + part).astype(jnp.bfloat16)
            g_sum[...] += jnp.dot(ht[:, at], rows, preferred_element_type=jnp.float32)

        def put(k, _):
            n = b * (BLK // GRP) + k
            pltpu.make_async_copy(
                d_buf.at[local_rows(n)], d_hbm.at[0, group_rows(hi, n)], sem.at[1]
            ).start()
            return 0

        lax.fori_loop(0, BLK // GRP, put, 0)
        return 0

    lax.fori_loop(0, 4, body, 0)
    g_buf[...] = g_sum[...].astype(jnp.bfloat16)
    second = pltpu.make_async_copy(g_buf, gd_hbm.at[0, :, pl.ds(last, 2 * LANES)], sem.at[2])
    second.start()
    first.wait()
    pltpu.make_async_copy(d_buf, d_hbm.at[0], sem.at[1]).wait()
    second.wait()


def per_device(grad_out, routes, probs, rows_hidden, w_down):
    bf = jnp.bfloat16
    any_spec = pl.BlockSpec(memory_space=pl.ANY)
    vmem = pl.BlockSpec(memory_space=pltpu.VMEM)
    kept = pl.pallas_call(
        gather_kernel,
        out_shape=(
            pltpu.VMEM(((4 - DONE) * BLK, 2 * LANES), bf),
            pltpu.VMEM((ROWS, FFD), jnp.float32),
            pltpu.VMEM((2, FFD, 2 * LANES), jnp.float32),
            pltpu.VMEM((FFD, D), bf),
            pltpu.VMEM((FFD, ROWS), bf),
            pltpu.VMEM((FFD, D), bf),
        ),
        in_specs=[any_spec] * 5,
        out_specs=[vmem] * 6,
        scratch_shapes=[
            pltpu.VMEM((2, TOK), jnp.int32),
            pltpu.VMEM((2, TOK), jnp.float32),
            pltpu.VMEM((COLS, ROWS, LANES), bf),
            pltpu.VMEM((COLS, EXPERTS * WIN, LANES), bf),
            pltpu.VMEM((COLS, 8, WIN, LANES), bf),
            pltpu.VMEM((ROWS, FFD), bf),
            pltpu.VMEM((TOK, D), bf),
            pltpu.VMEM((EXPERTS * WIN, TOK), bf),
            pltpu.VMEM((EXPERTS * WIN, LANES), jnp.float32),
            pltpu.SemaphoreType.DMA((2, NC)),
            pltpu.SemaphoreType.DMA((8, NC)),
            pltpu.SemaphoreType.DMA((5,)),
        ],
        compiler_params=pltpu.CompilerParams(
            collective_id=0, has_side_effects=True, vmem_limit_bytes=41 * 2**20
        ),
        cost_estimate=pl.CostEstimate(
            flops=4 * ROWS * D * FFD, bytes_accessed=2 * (2 * ROWS * FFD + 2 * FFD * D), transcendentals=0
        ),
    )(routes.T, probs.T, grad_out, rows_hidden, w_down)
    return pl.pallas_call(
        store_kernel,
        out_shape=(
            jax.ShapeDtypeStruct((1, ROWS, FFD), bf),
            jax.ShapeDtypeStruct((1, FFD, D), bf),
        ),
        in_specs=[vmem] * 6,
        out_specs=(any_spec, any_spec),
        scratch_shapes=[
            pltpu.VMEM((ROWS, FFD), bf),
            pltpu.VMEM((FFD, 2 * LANES), bf),
            pltpu.VMEM((FFD, 2 * LANES), jnp.float32),
            pltpu.SemaphoreType.DMA((3,)),
        ],
        compiler_params=pltpu.CompilerParams(vmem_limit_bytes=10 * 2**20),
    )(*(pltpu.with_memory_space_constraint(a, pltpu.VMEM) for a in kept))


def solution(mesh):
    return jax.shard_map(
        per_device,
        mesh=mesh,
        in_specs=(
            P(("rep", "exp"), None),
            P(("rep", "exp"), None),
            P(("rep", "exp"), None),
            P("exp", None, "rep"),
            P("exp", "rep", None),
        ),
        out_specs=(P("exp", None, "rep"), P("exp", "rep", None)),
        check_vma=False,
    )
```

```python
import jax
import jax.numpy as jnp
from jax import lax
from jax.experimental import pallas as pl
from jax.experimental.pallas import tpu as pltpu
from jax.sharding import PartitionSpec as P

CAP = 36
EXPERTS = 8
TOK = 128
D = 3072
FFD = 512
ROWS = 4608
LANES = 128
COLS = D // LANES
PAIRS = COLS // 2
HEAD, TAIL = 2, 2
NC = HEAD + (COLS - HEAD - TAIL) // 2 + TAIL
WIN = 48
GRP = 4 * CAP
UNIT = 2 * GRP
NU = 16
A = 160
A1 = 64
BR = UNIT - A
MESH = pl.DeviceIdType.MESH

LEXP, L1, L2, L3, LC1, LC2, LC3, LC4 = range(8)
BLK = 4 * UNIT
DONE = 2


def group_rows(hi, i):
    u, part = i // 2, i % 2
    g = (u + 8 * part) % 16 * 2 + (hi + part) % 2
    return pl.ds(pl.multiple_of(g * GRP, 16), GRP)


def local_rows(i):
    return pl.ds(pl.multiple_of(i * GRP, 16), GRP)


def block_rows(b):
    return pl.ds(pl.multiple_of(b * BLK, BLK), BLK)


def late_block(lo, y):
    return (1 - lo) * 2 + (y + 2) % 4 // 2


def gather_kernel(
    rt_hbm, pt_hbm, g_hbm, h_hbm, w_hbm, rows_out, acc, gacc, grad, ht, wv,
    rt_ref, pt_ref, dy, send, recv, hb, gv, sel, prow,
    ssem, rsem, lsem,
):
    rep = lax.axis_index("rep")
    ex = lax.axis_index("exp")
    lo, y, core = rep // 8, (rep // 2) % 4, rep % 2
    hi, z = ex // 4, ex % 4

    def unit(dl, dyy):
        return ((lo + dl) % 2 * 4 + (y + dyy + 4) % 4) * 2 + core

    to_x = (unit(1, 0), ex)
    to_yp = (unit(0, 1), ex)
    to_ym = (unit(0, -1), ex)
    to_core = ((lo * 4 + y) * 2 + 1 - core, ex)
    spread = []
    for dh in (1, 0):
        for dz in (2, 1, 3, 0):
            if dh or dz:
                hz = (hi + dh) % 2 * 4 + (z + dz) % 4
                spread.append((dh, (unit(dh, 0), hz), hz))
    peers = [to_x, to_yp, to_ym, to_core] + [s[1] for s in spread]

    load_g = pltpu.make_async_copy(g_hbm, gv, lsem.at[0])
    load_w = pltpu.make_async_copy(w_hbm.at[0], wv, lsem.at[1])
    load_r = pltpu.make_async_copy(rt_hbm, rt_ref, lsem.at[3])
    load_p = pltpu.make_async_copy(pt_hbm, pt_ref, lsem.at[4])
    load_r.start()
    load_p.start()
    load_g.start()

    bar = pltpu.get_barrier_semaphore()
    for p in peers:
        pl.semaphore_signal(bar, inc=1, device_id=p, device_id_type=MESH)

    def start_hidden(i, _):
        pltpu.make_async_copy(
            h_hbm.at[0, group_rows(hi, i)], hb.at[local_rows(i)], lsem.at[2]
        ).start()
        return 0

    load_r.wait()
    load_p.wait()
    rt = rt_ref[...]
    pt = pt_ref[...]
    erow = lax.broadcasted_iota(jnp.int32, (EXPERTS, TOK), 0)
    oh0 = (rt[0:1] == erow).astype(jnp.float32)
    oh1 = (rt[1:2] == erow).astype(jnp.float32)
    upper = (
        lax.broadcasted_iota(jnp.int32, (TOK, TOK), 0)
        < lax.broadcasted_iota(jnp.int32, (TOK, TOK), 1)
    ).astype(jnp.float32)
    before = jnp.dot(oh0 + oh1, upper, preferred_element_type=jnp.float32)
    slot0 = jnp.sum(oh0 * before, axis=0, keepdims=True).astype(jnp.int32)
    slot1 = jnp.sum(oh1 * before, axis=0, keepdims=True).astype(jnp.int32)
    t0 = rt[0:1] * WIN + slot0 + 4 * z
    t1 = rt[1:2] * WIN + slot1 + 4 * z
    row = lax.broadcasted_iota(jnp.int32, (EXPERTS * WIN, TOK), 0)
    m0 = row == t0
    m1 = row == t1
    sel[...] = (m0 | m1).astype(jnp.float32).astype(jnp.bfloat16)
    pw = jnp.where(m0, pt[0:1], 0.0) + jnp.where(m1, pt[1:2], 0.0)
    prow[...] = jnp.broadcast_to(jnp.sum(pw, axis=1, keepdims=True), prow.shape)

    def tile0(c):
        return jnp.where(c < HEAD, c, jnp.where(c < NC - TAIL, 2 * c - HEAD, c + COLS - NC))

    def wide(c, fn):
        one = (c < HEAD) | (c >= NC - TAIL)

        @pl.when(one)
        def _():
            fn(c, 1)

        @pl.when(jnp.logical_not(one))
        def _():
            fn(c, 2)

    def remote(src, dst, stage, c, device):
        s = 0 if stage == LEXP else 1
        pltpu.make_async_remote_copy(
            src_ref=src, dst_ref=dst, send_sem=ssem.at[s, c], recv_sem=rsem.at[stage, c],
            device_id=device, device_id_type=MESH,
        ).start()

    def wait_rows(sem, c, n, rows):
        ref = dy.at[pl.ds(tile0(c), n), pl.ds(0, rows)]
        pltpu.make_async_copy(ref, ref, sem).wait()

    def wait_windows(sem, c, n):
        ref = recv.at[pl.ds(tile0(c), n), pl.ds(0, 7)]
        pltpu.make_async_copy(ref, ref, sem).wait()

    def push(stage, c, n, u, start, rows, device):
        ref = dy.at[pl.ds(tile0(c), n), pl.ds(pl.multiple_of(u * UNIT + start, 16), rows)]
        remote(ref, ref, stage, c, device)

    def make_windows(c, n):
        g = gv[:, pl.ds(pl.multiple_of(tile0(c) * LANES, LANES), n * LANES)]
        rows = jnp.dot(sel[...], g, preferred_element_type=jnp.float32)
        for i in range(n):
            tile = rows[:, i * LANES : (i + 1) * LANES] * prow[...]
            send[tile0(c) + i] = tile.astype(jnp.bfloat16)

    def send_windows(c, n):
        for dh, device, e in spread:
            remote(
                send.at[pl.ds(tile0(c), n), pl.ds(pl.multiple_of(e * WIN, 16), WIN)],
                recv.at[pl.ds(tile0(c), n), dh * 4 + z],
                LEXP, c, device,
            )
        for i in range(n):
            recv[tile0(c) + i, z] = send[tile0(c) + i, pl.ds(pl.multiple_of(ex * WIN, 16), WIN), :]

    def prep(c, n):
        make_windows(c, n)
        send_windows(c, n)

    def stage1(c, n):
        wait_windows(rsem.at[LEXP, c], c, n)
        for i in range(n):
            k = tile0(c) + i
            for part in range(2):
                for s in range(4):
                    at = rep * UNIT + part * GRP + s * 32
                    q = part * 4 + s
                    if s == 0:
                        first = recv[k, q, 0:16, :]
                    else:
                        first = recv[k, q - 1, 32:48, :] + recv[k, q, 0:16, :]
                    dy[k, pl.ds(pl.multiple_of(at, 16), 16), :] = first
                    dy[k, pl.ds(pl.multiple_of(at + 16, 16), 16), :] = recv[k, q, 16:32, :]
                    if s == 3:
                        dy[k, pl.ds(pl.multiple_of(at + 32, 16), 16), :] = recv[k, q, 32:48, :]
        for device in (to_x, to_yp, to_ym):
            push(L1, c, n, rep, 0, UNIT, device)
        push(LC1, c, n, rep, 0, UNIT, to_core)

    def stage2(c, n):
        wait_rows(rsem.at[L1, c], c, n, 3 * UNIT)
        push(L2, c, n, unit(0, -1), 0, A, to_yp)
        push(L2, c, n, unit(0, 1), A, BR, to_ym)
        push(L2, c, n, unit(0, 1), A, BR, to_x)
        push(L2, c, n, unit(1, 0), 0, A, to_yp)
        push(L2, c, n, unit(1, 0), 0, A, to_ym)
        push(L2, c, n, unit(0, -1), A, BR, to_x)
        for u in (unit(1, 0), unit(0, 1), unit(0, -1)):
            push(LC2, c, n, u, 0, UNIT, to_core)

    def stage3(c, n):
        wait_rows(rsem.at[L2, c], c, n, 3 * UNIT)
        push(L3, c, n, unit(1, -1), 0, A1, to_yp)
        push(L3, c, n, unit(1, 1), A1, A - A1, to_ym)
        push(L3, c, n, unit(0, 2), A, BR, to_x)
        for u in (unit(0, 2), unit(1, 1), unit(1, -1)):
            push(LC3, c, n, u, 0, UNIT, to_core)

    def stage4(c, n):
        wait_rows(rsem.at[L3, c], c, n, UNIT)
        push(LC4, c, n, unit(1, 2), 0, UNIT, to_core)

    def arrived(c, n):
        wait_rows(rsem.at[LC1, c], c, n, UNIT)
        wait_rows(rsem.at[LC2, c], c, n, 3 * UNIT)
        wait_rows(rsem.at[LC3, c], c, n, 3 * UNIT)

    def multiply(k, b):
        at = pl.ds(pl.multiple_of(b * BLK, BLK), BLK)
        rows = jnp.concatenate([dy[2 * k, at, :], dy[2 * k + 1, at, :]], axis=1)
        wc = wv[:, pl.ds(pl.multiple_of(k * 2 * LANES, 2 * LANES), 2 * LANES)]
        gacc[k % 2] += jnp.dot(ht[:, at], rows, preferred_element_type=jnp.float32)
        acc[at, :] += lax.dot_general(
            rows, wc, (((1,), (1,)), ((), ())), preferred_element_type=jnp.float32
        )

    late = late_block(lo, y)

    def completes(c):
        wide_c = (c >= HEAD) & (c < NC - TAIL)
        return (c >= 0) & (c < NC) & (wide_c | (tile0(c) % 2 == 1))

    def early(c):
        k = tile0(c) // 2
        gacc[k % 2] = jnp.zeros(gacc.shape[1:], jnp.float32)

        def body(i, _):
            @pl.when((c == NC - 3) & (i == 0))
            def _():
                stage2(NC - 1, 1)

            @pl.when((c == NC - 1) & (i == 1))
            def _():
                stage4(NC - 1, 1)

            multiply(k, (late + 1 + i) % 4)
            return 0

        lax.fori_loop(0, jnp.where(c == NC - 1, DONE, 3), body, 0)

    def finish(c, n):
        if n == 1:
            wait_rows(rsem.at[LC4, c - 1], c - 1, 1, UNIT)
        wait_rows(rsem.at[LC4, c], c, n, UNIT)
        k = tile0(c) // 2
        multiply(k, late)
        cols = pl.ds(pl.multiple_of(k * 2 * LANES, 2 * LANES), 2 * LANES)
        grad[:, cols] = gacc[k % 2].astype(jnp.bfloat16)

    def turn_hidden(part):
        def body(i, _):
            at = pl.ds(pl.multiple_of((part * 9 + i) * 128, 128), 128)
            ht[:, at] = hb[at, :].T
            return 0

        lax.fori_loop(0, 9, body, 0)

    load_g.wait()
    make_windows(0, 1)
    pl.semaphore_wait(bar, len(peers))
    send_windows(0, 1)
    lax.fori_loop(0, 32, start_hidden, 0)
    load_w.start()
    make_windows(1, 1)

    def clear(i, _):
        acc[block_rows(i), :] = jnp.zeros((BLK, FFD), jnp.float32)
        return 0

    lax.fori_loop(0, 4, clear, 0)
    send_windows(1, 1)
    make_windows(2, 2)

    def step(t, _):
        def stage(lag, fn, but=0):
            c = t - lag

            @pl.when((c >= 0) & (c < NC - but))
            def _():
                wide(c, fn)

        stage(0, stage1, 1)

        @pl.when(t == 0)
        def _():
            send_windows(2, 2)


        @pl.when((t > 0) & (t + 2 < NC))
        def _():
            wide(t + 2, prep)

        stage(1, stage2, 1)

        @pl.when(completes(t - 4) & (t < NC))
        def _():
            wide(t - 4, finish)

        stage(2, stage3)
        @pl.when(completes(t - 4) & (t == NC))
        def _():
            wide(t - 4, finish)

        stage(3, stage4, 1)

        @pl.when(t == NC - 2)
        def _():
            stage1(NC - 1, 1)

        @pl.when(t == 0)
        def _():
            pltpu.make_async_copy(hb, hb, lsem.at[2]).wait()
            load_w.wait()

        @pl.when(t < 4)
        def _():
            turn_hidden(t)

        stage(2, arrived)

        @pl.when(completes(t - 2))
        def _():
            early(t - 2)

        @pl.when(completes(t - 4) & (t == NC + 1))
        def _():
            wide(t - 4, finish)

        return 0

    lax.fori_loop(0, NC + 2, step, 0)
    for i in range(DONE, 4):
        if i == 3:
            for c in (NC - 2, NC - 1):
                wait_rows(rsem.at[LC4, c], c, 1, UNIT)
        at = block_rows((late + 1 + i) % 4)
        for k in range(2):
            rows_out[(i - DONE) * BLK : (i - DONE + 1) * BLK, k * LANES : (k + 1) * LANES] = dy[
                COLS - 2 + k, at, :
            ]

    def drain(c, _):
        def one(c, n):
            wait_windows(ssem.at[0, c], c, n)
            wait_rows(ssem.at[1, c], c, n, 15 * UNIT)

        wide(c, one)
        return 0

    lax.fori_loop(0, NC, drain, 0)


def store_kernel(rows_in, acc, gacc, grad, ht, wv, d_hbm, gd_hbm, d_buf, g_buf, g_sum, sem):
    rep, ex = lax.axis_index("rep"), lax.axis_index("exp")
    late, hi = late_block(rep // 8, (rep // 2) % 4), ex // 4
    last = (PAIRS - 1) * 2 * LANES
    first = pltpu.make_async_copy(grad.at[:, pl.ds(0, last)], gd_hbm.at[0, :, pl.ds(0, last)], sem.at[0])
    first.start()
    g_sum[...] = gacc[(PAIRS - 1) % 2]

    def body(i, _):
        b = (late + 1 + i) % 4
        at = block_rows(b)

        @pl.when(i < DONE)
        def _():
            d_buf[at, :] = acc[at, :].astype(jnp.bfloat16)

        @pl.when(i >= DONE)
        def _():
            rows = rows_in[block_rows(i - DONE), :]
            part = lax.dot_general(
                rows, wv[:, last:], (((1,), (1,)), ((), ())), preferred_element_type=jnp.float32
            )
            d_buf[at, :] = (acc[at, :] + part).astype(jnp.bfloat16)
            g_sum[...] += jnp.dot(ht[:, at], rows, preferred_element_type=jnp.float32)

        def put(k, _):
            n = b * (BLK // GRP) + k
            pltpu.make_async_copy(
                d_buf.at[local_rows(n)], d_hbm.at[0, group_rows(hi, n)], sem.at[1]
            ).start()
            return 0

        lax.fori_loop(0, BLK // GRP, put, 0)
        return 0

    lax.fori_loop(0, 4, body, 0)
    g_buf[...] = g_sum[...].astype(jnp.bfloat16)
    second = pltpu.make_async_copy(g_buf, gd_hbm.at[0, :, pl.ds(last, 2 * LANES)], sem.at[2])
    second.start()
    first.wait()
    pltpu.make_async_copy(d_buf, d_hbm.at[0], sem.at[1]).wait()
    second.wait()


def per_device(grad_out, routes, probs, rows_hidden, w_down):
    bf = jnp.bfloat16
    any_spec = pl.BlockSpec(memory_space=pl.ANY)
    vmem = pl.BlockSpec(memory_space=pltpu.VMEM)
    kept = pl.pallas_call(
        gather_kernel,
        out_shape=(
            pltpu.VMEM(((4 - DONE) * BLK, 2 * LANES), bf),
            pltpu.VMEM((ROWS, FFD), jnp.float32),
            pltpu.VMEM((2, FFD, 2 * LANES), jnp.float32),
            pltpu.VMEM((FFD, D), bf),
            pltpu.VMEM((FFD, ROWS), bf),
            pltpu.VMEM((FFD, D), bf),
        ),
        in_specs=[any_spec] * 5,
        out_specs=[vmem] * 6,
        scratch_shapes=[
            pltpu.VMEM((2, TOK), jnp.int32),
            pltpu.VMEM((2, TOK), jnp.float32),
            pltpu.VMEM((COLS, ROWS, LANES), bf),
            pltpu.VMEM((COLS, EXPERTS * WIN, LANES), bf),
            pltpu.VMEM((COLS, 8, WIN, LANES), bf),
            pltpu.VMEM((ROWS, FFD), bf),
            pltpu.VMEM((TOK, D), bf),
            pltpu.VMEM((EXPERTS * WIN, TOK), bf),
            pltpu.VMEM((EXPERTS * WIN, LANES), jnp.float32),
            pltpu.SemaphoreType.DMA((2, NC)),
            pltpu.SemaphoreType.DMA((8, NC)),
            pltpu.SemaphoreType.DMA((5,)),
        ],
        compiler_params=pltpu.CompilerParams(
            collective_id=0, has_side_effects=True, vmem_limit_bytes=41 * 2**20
        ),
        cost_estimate=pl.CostEstimate(
            flops=4 * ROWS * D * FFD, bytes_accessed=2 * (2 * ROWS * FFD + 2 * FFD * D), transcendentals=0
        ),
    )(routes.T, probs.T, grad_out, rows_hidden, w_down)
    return pl.pallas_call(
        store_kernel,
        out_shape=(
            jax.ShapeDtypeStruct((1, ROWS, FFD), bf),
            jax.ShapeDtypeStruct((1, FFD, D), bf),
        ),
        in_specs=[vmem] * 6,
        out_specs=(any_spec, any_spec),
        scratch_shapes=[
            pltpu.VMEM((ROWS, FFD), bf),
            pltpu.VMEM((FFD, 2 * LANES), bf),
            pltpu.VMEM((FFD, 2 * LANES), jnp.float32),
            pltpu.SemaphoreType.DMA((3,)),
        ],
        compiler_params=pltpu.CompilerParams(vmem_limit_bytes=10 * 2**20),
    )(*(pltpu.with_memory_space_constraint(a, pltpu.VMEM) for a in kept))


def solution(mesh):
    return jax.shard_map(
        per_device,
        mesh=mesh,
        in_specs=(
            P(("rep", "exp"), None),
            P(("rep", "exp"), None),
            P(("rep", "exp"), None),
            P("exp", None, "rep"),
            P("exp", "rep", None),
        ),
        out_specs=(P("exp", None, "rep"), P("exp", "rep", None)),
        check_vma=False,
    )
```

```python
import jax
import jax.numpy as jnp
from jax import lax
from jax.experimental import pallas as pl
from jax.experimental.pallas import tpu as pltpu
from jax.sharding import PartitionSpec as P

CAP = 36
EXPERTS = 8
TOK = 128
D = 3072
FFD = 512
ROWS = 4608
LANES = 128
COLS = D // LANES
PAIRS = COLS // 2
HEAD, TAIL = 2, 2
NC = HEAD + (COLS - HEAD - TAIL) // 2 + TAIL
WIN = 48
GRP = 4 * CAP
UNIT = 2 * GRP
NU = 16
A = 160
A1 = 64
BR = UNIT - A
MESH = pl.DeviceIdType.MESH

LEXP, L1, L2, L3, LC1, LC2, LC3, LC4 = range(8)
BLK = 4 * UNIT
DONE = 2


def group_rows(hi, i):
    u, part = i // 2, i % 2
    g = (u + 8 * part) % 16 * 2 + (hi + part) % 2
    return pl.ds(pl.multiple_of(g * GRP, 16), GRP)


def local_rows(i):
    return pl.ds(pl.multiple_of(i * GRP, 16), GRP)


def block_rows(b):
    return pl.ds(pl.multiple_of(b * BLK, BLK), BLK)


def late_block(lo, y):
    return (1 - lo) * 2 + (y + 2) % 4 // 2


def gather_kernel(
    rt_hbm, pt_hbm, g_hbm, h_hbm, w_hbm, rows_out, acc, gacc, grad, ht, wv,
    rt_ref, pt_ref, dy, send, recv, hb, gv, sel, prow,
    ssem, rsem, lsem,
):
    rep = lax.axis_index("rep")
    ex = lax.axis_index("exp")
    lo, y, core = rep // 8, (rep // 2) % 4, rep % 2
    hi, z = ex // 4, ex % 4

    def unit(dl, dyy):
        return ((lo + dl) % 2 * 4 + (y + dyy + 4) % 4) * 2 + core

    to_x = (unit(1, 0), ex)
    to_yp = (unit(0, 1), ex)
    to_ym = (unit(0, -1), ex)
    to_core = ((lo * 4 + y) * 2 + 1 - core, ex)
    spread = []
    for dh in (1, 0):
        for dz in (2, 1, 3, 0):
            if dh or dz:
                hz = (hi + dh) % 2 * 4 + (z + dz) % 4
                spread.append((dh, (unit(dh, 0), hz), hz))
    peers = [to_x, to_yp, to_ym, to_core] + [s[1] for s in spread]

    load_g = pltpu.make_async_copy(g_hbm, gv, lsem.at[0])
    load_w = pltpu.make_async_copy(w_hbm.at[0], wv, lsem.at[1])
    load_r = pltpu.make_async_copy(rt_hbm, rt_ref, lsem.at[3])
    load_p = pltpu.make_async_copy(pt_hbm, pt_ref, lsem.at[4])
    load_r.start()
    load_p.start()
    load_g.start()

    bar = pltpu.get_barrier_semaphore()
    for p in peers:
        pl.semaphore_signal(bar, inc=1, device_id=p, device_id_type=MESH)

    def start_hidden(i, _):
        pltpu.make_async_copy(
            h_hbm.at[0, group_rows(hi, i)], hb.at[local_rows(i)], lsem.at[2]
        ).start()
        return 0

    load_r.wait()
    load_p.wait()
    rt = rt_ref[...]
    pt = pt_ref[...]
    erow = lax.broadcasted_iota(jnp.int32, (EXPERTS, TOK), 0)
    oh0 = (rt[0:1] == erow).astype(jnp.float32)
    oh1 = (rt[1:2] == erow).astype(jnp.float32)
    upper = (
        lax.broadcasted_iota(jnp.int32, (TOK, TOK), 0)
        < lax.broadcasted_iota(jnp.int32, (TOK, TOK), 1)
    ).astype(jnp.float32)
    before = jnp.dot(oh0 + oh1, upper, preferred_element_type=jnp.float32)
    slot0 = jnp.sum(oh0 * before, axis=0, keepdims=True).astype(jnp.int32)
    slot1 = jnp.sum(oh1 * before, axis=0, keepdims=True).astype(jnp.int32)
    t0 = rt[0:1] * WIN + slot0 + 4 * z
    t1 = rt[1:2] * WIN + slot1 + 4 * z
    row = lax.broadcasted_iota(jnp.int32, (EXPERTS * WIN, TOK), 0)
    m0 = row == t0
    m1 = row == t1
    sel[...] = (m0 | m1).astype(jnp.float32).astype(jnp.bfloat16)
    pw = jnp.where(m0, pt[0:1], 0.0) + jnp.where(m1, pt[1:2], 0.0)
    prow[...] = jnp.broadcast_to(jnp.sum(pw, axis=1, keepdims=True), prow.shape)

    def tile0(c):
        return jnp.where(c < HEAD, c, jnp.where(c < NC - TAIL, 2 * c - HEAD, c + COLS - NC))

    def wide(c, fn):
        one = (c < HEAD) | (c >= NC - TAIL)

        @pl.when(one)
        def _():
            fn(c, 1)

        @pl.when(jnp.logical_not(one))
        def _():
            fn(c, 2)

    def remote(src, dst, stage, c, device):
        s = 0 if stage == LEXP else 1
        pltpu.make_async_remote_copy(
            src_ref=src, dst_ref=dst, send_sem=ssem.at[s, c], recv_sem=rsem.at[stage, c],
            device_id=device, device_id_type=MESH,
        ).start()

    def wait_rows(sem, c, n, rows):
        ref = dy.at[pl.ds(tile0(c), n), pl.ds(0, rows)]
        pltpu.make_async_copy(ref, ref, sem).wait()

    def wait_windows(sem, c, n):
        ref = recv.at[pl.ds(tile0(c), n), pl.ds(0, 7)]
        pltpu.make_async_copy(ref, ref, sem).wait()

    def push(stage, c, n, u, start, rows, device):
        ref = dy.at[pl.ds(tile0(c), n), pl.ds(pl.multiple_of(u * UNIT + start, 16), rows)]
        remote(ref, ref, stage, c, device)

    def make_windows(c, n):
        g = gv[:, pl.ds(pl.multiple_of(tile0(c) * LANES, LANES), n * LANES)]
        rows = jnp.dot(sel[...], g, preferred_element_type=jnp.float32)
        for i in range(n):
            tile = rows[:, i * LANES : (i + 1) * LANES] * prow[...]
            send[tile0(c) + i] = tile.astype(jnp.bfloat16)

    def send_windows(c, n):
        for dh, device, e in spread:
            remote(
                send.at[pl.ds(tile0(c), n), pl.ds(pl.multiple_of(e * WIN, 16), WIN)],
                recv.at[pl.ds(tile0(c), n), dh * 4 + z],
                LEXP, c, device,
            )
        for i in range(n):
            recv[tile0(c) + i, z] = send[tile0(c) + i, pl.ds(pl.multiple_of(ex * WIN, 16), WIN), :]

    def prep(c, n):
        make_windows(c, n)
        send_windows(c, n)

    def stage1(c, n):
        wait_windows(rsem.at[LEXP, c], c, n)
        for i in range(n):
            k = tile0(c) + i
            for part in range(2):
                for s in range(4):
                    at = rep * UNIT + part * GRP + s * 32
                    q = part * 4 + s
                    if s == 0:
                        first = recv[k, q, 0:16, :]
                    else:
                        first = recv[k, q - 1, 32:48, :] + recv[k, q, 0:16, :]
                    dy[k, pl.ds(pl.multiple_of(at, 16), 16), :] = first
                    dy[k, pl.ds(pl.multiple_of(at + 16, 16), 16), :] = recv[k, q, 16:32, :]
                    if s == 3:
                        dy[k, pl.ds(pl.multiple_of(at + 32, 16), 16), :] = recv[k, q, 32:48, :]
        for device in (to_x, to_yp, to_ym):
            push(L1, c, n, rep, 0, UNIT, device)
        push(LC1, c, n, rep, 0, UNIT, to_core)

    def stage2(c, n):
        wait_rows(rsem.at[L1, c], c, n, 3 * UNIT)
        push(L2, c, n, unit(0, -1), 0, A, to_yp)
        push(L2, c, n, unit(0, 1), A, BR, to_ym)
        push(L2, c, n, unit(0, 1), A, BR, to_x)
        push(L2, c, n, unit(1, 0), 0, A, to_yp)
        push(L2, c, n, unit(1, 0), 0, A, to_ym)
        push(L2, c, n, unit(0, -1), A, BR, to_x)
        for u in (unit(1, 0), unit(0, 1), unit(0, -1)):
            push(LC2, c, n, u, 0, UNIT, to_core)

    def stage3(c, n):
        wait_rows(rsem.at[L2, c], c, n, 3 * UNIT)
        push(L3, c, n, unit(1, -1), 0, A1, to_yp)
        push(L3, c, n, unit(1, 1), A1, A - A1, to_ym)
        push(L3, c, n, unit(0, 2), A, BR, to_x)
        for u in (unit(0, 2), unit(1, 1), unit(1, -1)):
            push(LC3, c, n, u, 0, UNIT, to_core)

    def stage4(c, n):
        wait_rows(rsem.at[L3, c], c, n, UNIT)
        push(LC4, c, n, unit(1, 2), 0, UNIT, to_core)

    def arrived(c, n):
        wait_rows(rsem.at[LC1, c], c, n, UNIT)
        wait_rows(rsem.at[LC2, c], c, n, 3 * UNIT)
        wait_rows(rsem.at[LC3, c], c, n, 3 * UNIT)

    def multiply(k, b):
        at = pl.ds(pl.multiple_of(b * BLK, BLK), BLK)
        rows = jnp.concatenate([dy[2 * k, at, :], dy[2 * k + 1, at, :]], axis=1)
        wc = wv[:, pl.ds(pl.multiple_of(k * 2 * LANES, 2 * LANES), 2 * LANES)]
        gacc[k % 2] += jnp.dot(ht[:, at], rows, preferred_element_type=jnp.float32)
        acc[at, :] += lax.dot_general(
            rows, wc, (((1,), (1,)), ((), ())), preferred_element_type=jnp.float32
        )

    late = late_block(lo, y)

    def completes(c):
        wide_c = (c >= HEAD) & (c < NC - TAIL)
        return (c >= 0) & (c < NC) & (wide_c | (tile0(c) % 2 == 1))

    def early(c):
        k = tile0(c) // 2
        gacc[k % 2] = jnp.zeros(gacc.shape[1:], jnp.float32)

        def body(i, _):
            @pl.when((c == NC - 3) & (i == 0))
            def _():
                stage2(NC - 1, 1)

            multiply(k, (late + 1 + i) % 4)
            return 0

        lax.fori_loop(0, jnp.where(c == NC - 1, DONE, 3), body, 0)

    def finish(c, n):
        if n == 1:
            wait_rows(rsem.at[LC4, c - 1], c - 1, 1, UNIT)
        wait_rows(rsem.at[LC4, c], c, n, UNIT)
        k = tile0(c) // 2
        multiply(k, late)
        cols = pl.ds(pl.multiple_of(k * 2 * LANES, 2 * LANES), 2 * LANES)
        grad[:, cols] = gacc[k % 2].astype(jnp.bfloat16)

    def turn_hidden(part):
        def body(i, _):
            at = pl.ds(pl.multiple_of((part * 9 + i) * 128, 128), 128)
            ht[:, at] = hb[at, :].T
            return 0

        lax.fori_loop(0, 9, body, 0)

    load_g.wait()
    make_windows(0, 1)
    pl.semaphore_wait(bar, len(peers))
    send_windows(0, 1)
    lax.fori_loop(0, 32, start_hidden, 0)
    load_w.start()
    make_windows(1, 1)

    def clear(i, _):
        acc[block_rows(i), :] = jnp.zeros((BLK, FFD), jnp.float32)
        return 0

    lax.fori_loop(0, 4, clear, 0)
    send_windows(1, 1)
    make_windows(2, 2)

    def step(t, _):
        def stage(lag, fn, but=0):
            c = t - lag

            @pl.when((c >= 0) & (c < NC - but))
            def _():
                wide(c, fn)

        stage(0, stage1, 1)

        @pl.when(t == 0)
        def _():
            send_windows(2, 2)


        @pl.when((t > 0) & (t + 2 < NC))
        def _():
            wide(t + 2, prep)

        stage(1, stage2, 1)

        @pl.when(completes(t - 4) & (t < NC))
        def _():
            wide(t - 4, finish)

        stage(2, stage3)
        @pl.when(completes(t - 4) & (t == NC))
        def _():
            wide(t - 4, finish)

        stage(3, stage4, 1)

        @pl.when(t == NC - 2)
        def _():
            stage1(NC - 1, 1)

        @pl.when(t == 0)
        def _():
            pltpu.make_async_copy(hb, hb, lsem.at[2]).wait()
            load_w.wait()

        @pl.when(t < 4)
        def _():
            turn_hidden(t)

        stage(2, arrived)

        @pl.when(completes(t - 2))
        def _():
            early(t - 2)

        @pl.when(t == NC + 1)
        def _():
            stage4(NC - 1, 1)

        @pl.when(completes(t - 4) & (t == NC + 1))
        def _():
            wide(t - 4, finish)

        return 0

    lax.fori_loop(0, NC + 2, step, 0)
    for i in range(DONE, 4):
        if i == 3:
            for c in (NC - 2, NC - 1):
                wait_rows(rsem.at[LC4, c], c, 1, UNIT)
        at = block_rows((late + 1 + i) % 4)
        for k in range(2):
            rows_out[(i - DONE) * BLK : (i - DONE + 1) * BLK, k * LANES : (k + 1) * LANES] = dy[
                COLS - 2 + k, at, :
            ]

    def drain(c, _):
        def one(c, n):
            wait_windows(ssem.at[0, c], c, n)
            wait_rows(ssem.at[1, c], c, n, 15 * UNIT)

        wide(c, one)
        return 0

    lax.fori_loop(0, NC, drain, 0)


def store_kernel(rows_in, acc, gacc, grad, ht, wv, d_hbm, gd_hbm, d_buf, g_buf, g_sum, sem):
    rep, ex = lax.axis_index("rep"), lax.axis_index("exp")
    late, hi = late_block(rep // 8, (rep // 2) % 4), ex // 4
    last = (PAIRS - 1) * 2 * LANES
    first = pltpu.make_async_copy(grad.at[:, pl.ds(0, last)], gd_hbm.at[0, :, pl.ds(0, last)], sem.at[0])
    first.start()
    g_sum[...] = gacc[(PAIRS - 1) % 2]

    def body(i, _):
        b = (late + 1 + i) % 4
        at = block_rows(b)

        @pl.when(i < DONE)
        def _():
            d_buf[at, :] = acc[at, :].astype(jnp.bfloat16)

        @pl.when(i >= DONE)
        def _():
            rows = rows_in[block_rows(i - DONE), :]
            part = lax.dot_general(
                rows, wv[:, last:], (((1,), (1,)), ((), ())), preferred_element_type=jnp.float32
            )
            d_buf[at, :] = (acc[at, :] + part).astype(jnp.bfloat16)
            g_sum[...] += jnp.dot(ht[:, at], rows, preferred_element_type=jnp.float32)

        def put(k, _):
            n = b * (BLK // GRP) + k
            pltpu.make_async_copy(
                d_buf.at[local_rows(n)], d_hbm.at[0, group_rows(hi, n)], sem.at[1]
            ).start()
            return 0

        lax.fori_loop(0, BLK // GRP, put, 0)
        return 0

    lax.fori_loop(0, 4, body, 0)
    g_buf[...] = g_sum[...].astype(jnp.bfloat16)
    second = pltpu.make_async_copy(g_buf, gd_hbm.at[0, :, pl.ds(last, 2 * LANES)], sem.at[2])
    second.start()
    first.wait()
    pltpu.make_async_copy(d_buf, d_hbm.at[0], sem.at[1]).wait()
    second.wait()


def per_device(grad_out, routes, probs, rows_hidden, w_down):
    bf = jnp.bfloat16
    any_spec = pl.BlockSpec(memory_space=pl.ANY)
    vmem = pl.BlockSpec(memory_space=pltpu.VMEM)
    kept = pl.pallas_call(
        gather_kernel,
        out_shape=(
            pltpu.VMEM(((4 - DONE) * BLK, 2 * LANES), bf),
            pltpu.VMEM((ROWS, FFD), jnp.float32),
            pltpu.VMEM((2, FFD, 2 * LANES), jnp.float32),
            pltpu.VMEM((FFD, D), bf),
            pltpu.VMEM((FFD, ROWS), bf),
            pltpu.VMEM((FFD, D), bf),
        ),
        in_specs=[any_spec] * 5,
        out_specs=[vmem] * 6,
        scratch_shapes=[
            pltpu.VMEM((2, TOK), jnp.int32),
            pltpu.VMEM((2, TOK), jnp.float32),
            pltpu.VMEM((COLS, ROWS, LANES), bf),
            pltpu.VMEM((COLS, EXPERTS * WIN, LANES), bf),
            pltpu.VMEM((COLS, 8, WIN, LANES), bf),
            pltpu.VMEM((ROWS, FFD), bf),
            pltpu.VMEM((TOK, D), bf),
            pltpu.VMEM((EXPERTS * WIN, TOK), bf),
            pltpu.VMEM((EXPERTS * WIN, LANES), jnp.float32),
            pltpu.SemaphoreType.DMA((2, NC)),
            pltpu.SemaphoreType.DMA((8, NC)),
            pltpu.SemaphoreType.DMA((5,)),
        ],
        compiler_params=pltpu.CompilerParams(
            collective_id=0, has_side_effects=True, vmem_limit_bytes=41 * 2**20
        ),
        cost_estimate=pl.CostEstimate(
            flops=4 * ROWS * D * FFD, bytes_accessed=2 * (2 * ROWS * FFD + 2 * FFD * D), transcendentals=0
        ),
    )(routes.T, probs.T, grad_out, rows_hidden, w_down)
    return pl.pallas_call(
        store_kernel,
        out_shape=(
            jax.ShapeDtypeStruct((1, ROWS, FFD), bf),
            jax.ShapeDtypeStruct((1, FFD, D), bf),
        ),
        in_specs=[vmem] * 6,
        out_specs=(any_spec, any_spec),
        scratch_shapes=[
            pltpu.VMEM((ROWS, FFD), bf),
            pltpu.VMEM((FFD, 2 * LANES), bf),
            pltpu.VMEM((FFD, 2 * LANES), jnp.float32),
            pltpu.SemaphoreType.DMA((3,)),
        ],
        compiler_params=pltpu.CompilerParams(vmem_limit_bytes=10 * 2**20),
    )(*(pltpu.with_memory_space_constraint(a, pltpu.VMEM) for a in kept))


def solution(mesh):
    return jax.shard_map(
        per_device,
        mesh=mesh,
        in_specs=(
            P(("rep", "exp"), None),
            P(("rep", "exp"), None),
            P(("rep", "exp"), None),
            P("exp", None, "rep"),
            P("exp", "rep", None),
        ),
        out_specs=(P("exp", None, "rep"), P("exp", "rep", None)),
        check_vma=False,
    )
```
